32 devices in a mesh: tm: 8 (over y, x, core), batch: 4 (over z).
Axes of the slice: x: 2, y: 2, z: 4, core: 2. Of those that a mesh axis runs over, the one named last changes fastest.
Arguments:
- rgb_maps: bfloat16 [16, 64, 16, 16, 128], P('batch', 'tm'), may hold values from -6 to 6
- flow_maps: bfloat16 [16, 64, 16, 16, 128], P('batch', 'tm'), may hold values from -6 to 6
- in_weights: bfloat16 [2, 1152, 128], replicated, may hold values from -0.1875 to 0.1875
- out_weights: bfloat16 [2, 1152, 128], replicated, may hold values from -0.1875 to 0.1875
- decay: float32 [2, 64, 128], P(None, 'tm'), may hold values from 0 to 1, as said below
- skip: float32 [2, 128], replicated, may hold values from 0.5 to 1.5
- proj_in: float32 [128, 2048], replicated, may hold values from -0.5 to 0.5
- proj_gain: float32 [2048], replicated, may hold values from 0.1 to 1.9
- proj_out: bfloat16 [2048, 2048], replicated, may hold values from -0.125 to 0.125
Outputs:
- grad_in: float32 [2, 1152, 128], replicated
- grad_out: float32 [2, 1152, 128], replicated
The draws below stay inside these ranges and needn't reach their ends.
Inputs may be any that keep to these rules, and one draw needn't show every extreme that they name: Every entry of decay is a retention factor between 0 and 1.
All inputs are finite; a program needn't handle non-finite values.
Results may differ from the reference program's by a relative error of at most 0.015.
The reference program's roundings to bfloat16 on the way count: a program that leaves them out, or rounds other values in their place, can miss the bound.
Values may be sent and summed in bfloat16 or wider, within the bound.
A program may use at most 256 MiB of HBM per device.

```python
import jax
import jax.numpy as jnp
from jax import lax

LAYER_CHANNELS = 128
PROJ = 2048
MAP = 16
CLIP_FRAMES = 64
CLIPS = 16


def draw_decay(key, part):
    random_keys = jax.random.split(jax.random.fold_in(key, 7), 6)
    fast_share = 0.45
    fast_pick = jax.random.uniform(random_keys[0], (2, LAYER_CHANNELS)) < fast_share
    slow_rate = jnp.exp(jax.random.uniform(random_keys[1], (2, LAYER_CHANNELS), minval=jnp.log(0.02), maxval=jnp.log(0.4))) / CLIP_FRAMES
    fast_rate = jnp.exp(jax.random.uniform(random_keys[2], (2, LAYER_CHANNELS), minval=jnp.log(0.06), maxval=jnp.log(0.12)))
    rate_base = jnp.where(fast_pick, fast_rate, slow_rate)
    jitter = jax.random.uniform(random_keys[3], (2, CLIP_FRAMES, LAYER_CHANNELS), minval=0.5, maxval=1.5)
    spike_positions = jax.random.randint(random_keys[4], (2, 4, LAYER_CHANNELS), 0, CLIP_FRAMES)
    frame_numbers = jnp.arange(CLIP_FRAMES)
    spike_mask = jnp.any(frame_numbers[None, :, None, None] == spike_positions[:, None, :, :], axis=2)
    spike_multiplier = jax.random.uniform(random_keys[5], (2, CLIP_FRAMES, LAYER_CHANNELS), minval=0.5, maxval=0.8)
    memory_keep = jnp.exp(-rate_base[:, None, :] * jitter)
    memory_keep = memory_keep * jnp.where(spike_mask, spike_multiplier, 1.0)
    return memory_keep.astype(jnp.float32)


def block_scale(stream_key, shape, cuts, smallest, top_value):
    def one(position, shards_of):
        heights = jax.random.uniform(jax.random.fold_in(jax.random.fold_in(stream_key, 6), position), (shards_of,), jnp.float32, smallest / len(cuts), top_value / len(cuts))
        return jnp.repeat(jnp.exp(heights), shape[position] // shards_of).reshape((-1,) + (1,) * (len(shape) - position - 1))

    level = one(*cuts[0])
    for cut in cuts[1:]:
        level = level * one(*cut)
    return level


def centred(stream_key, dims, deviation, reach, cuts=(), dtype=jnp.bfloat16):
    drawn = jax.random.normal(stream_key, dims, jnp.float32) * deviation
    if len(cuts) > 0:
        drawn = block_scale(stream_key, dims, cuts, -0.22, 0.18) * drawn
    return jnp.clip(drawn, min=-reach, max=reach).astype(dtype)


def setup_inputs(seed: int = 0) -> dict:
    key_list = jax.random.split(jax.random.key(seed), 10)
    rgb_maps = centred(key_list[0], (CLIPS, CLIP_FRAMES, MAP, MAP, LAYER_CHANNELS), 1.0, 6.0, ((0, 4), (1, 8)))
    flow_maps = centred(key_list[1], (CLIPS, CLIP_FRAMES, MAP, MAP, LAYER_CHANNELS), 1.0, 6.0, ((0, 4), (1, 8)))
    in_weights = centred(key_list[2], (2, 9 * LAYER_CHANNELS, LAYER_CHANNELS), (9 * LAYER_CHANNELS) ** -0.5, 0.1875)
    out_weights = centred(key_list[3], (2, 9 * LAYER_CHANNELS, LAYER_CHANNELS), (9 * LAYER_CHANNELS) ** -0.5, 0.1875)
    decay = draw_decay(jax.random.fold_in(key_list[9], 71), 0)
    skip = jnp.clip(jax.random.uniform(key_list[5], (2, LAYER_CHANNELS), jnp.float32, 0.5, 1.5), 0.5, 1.5)
    proj_in = centred(key_list[6], (LAYER_CHANNELS, PROJ), LAYER_CHANNELS ** -0.5, 0.5, (), jnp.float32)
    proj_gain = jnp.clip(1.0 + 0.18 * jax.random.normal(key_list[7], (PROJ,), jnp.float32), 0.1, 1.9)
    proj_out = centred(key_list[8], (PROJ, PROJ), PROJ ** -0.5, 0.125)
    return dict(rgb_maps=rgb_maps, flow_maps=flow_maps, in_weights=in_weights, out_weights=out_weights, decay=decay, skip=skip, proj_in=proj_in, proj_gain=proj_gain, proj_out=proj_out)


LAMBDA_OFF = 0.0051
EPSILON = 1e-05
HIGHEST = lax.Precision.HIGHEST

def patches(feature_maps, flip_sign):
    map_side = feature_maps.shape[-2]
    padding = [(0, 0)] * (feature_maps.ndim - 3) + [(1, 1), (1, 1), (0, 0)]
    padded = jnp.pad(feature_maps, padding)
    pieces = []
    for row_off in range(3):
        for col_off in range(3):
            top_row = 1 + flip_sign * (row_off - 1)
            left_col = 1 + flip_sign * (col_off - 1)
            pieces.append(padded[..., top_row:top_row + map_side, left_col:left_col + map_side, :])
    return jnp.concatenate(pieces, axis=-1)

def convolve(feature_maps, weights, flip_sign):
    stacked = patches(feature_maps, flip_sign)
    flat = stacked.reshape(-1, stacked.shape[-1])
    result = jnp.dot(flat, weights, preferred_element_type=jnp.float32)
    return result.reshape(feature_maps.shape[:-1] + (weights.shape[1],))

def flipped(weights):
    channels = weights.shape[1]
    return weights.reshape(9, channels, channels).transpose(0, 2, 1).reshape(9 * channels, channels)

def weight_product(feature_maps, grads):
    stacked = patches(feature_maps, 1)
    flat = stacked.reshape(-1, stacked.shape[-1])
    return lax.dot_general(flat, grads.reshape(-1, grads.shape[-1]), (((0,), (0,)), ((), ())), preferred_element_type=jnp.float32)

def silu_grad(values):
    sigma = jax.nn.sigmoid(values)
    return sigma * (1.0 + values * (1.0 - sigma))

def view_forward(clip_maps, in_w, out_w, decays, skip_v):
    inputs = convolve(clip_maps, in_w, 1).astype(jnp.bfloat16)

    def advance(carried, pair_in):
        decay_now, input_now = pair_in
        carried = decay_now * carried + input_now.astype(jnp.float32)
        return (carried, carried)
    start_state = jnp.zeros(clip_maps.shape[1:], jnp.float32)
    _, states = lax.scan(advance, start_state, (decays, inputs))
    states_b = states.astype(jnp.bfloat16)
    mixed_out = convolve(states_b, out_w, 1) + skip_v * inputs.astype(jnp.float32)
    return (inputs, states_b, mixed_out)

def batch_norm(values):
    center = lax.optimization_barrier(jnp.mean(values, axis=0))
    centered = values - center
    scale = lax.rsqrt(lax.optimization_barrier(jnp.mean(centered * centered, axis=0)) + EPSILON)
    return (centered * scale, scale)

def reference(rgb_maps, flow_maps, in_weights, out_weights, decay, skip, proj_in, proj_gain, proj_out):
    views = (rgb_maps, flow_maps)
    cell_count = rgb_maps.shape[1] * rgb_maps.shape[2] * rgb_maps.shape[3]
    clip_total = rgb_maps.shape[0]
    pooled_all = []
    for view_idx in range(2):

        def pool_clip(clip_maps, view_idx=view_idx):
            _, _, mixed_out = view_forward(clip_maps, in_weights[view_idx], out_weights[view_idx], decay[view_idx], skip[view_idx])
            return lax.optimization_barrier(jnp.sum(jax.nn.silu(mixed_out), axis=(0, 1, 2))) / cell_count
        pooled_all.append(lax.map(pool_clip, views[view_idx]))
    hidden_x, hidden_s, hidden_n, z_x, z_s, z_n = ([], [], [], [], [], [])
    for view_idx in range(2):
        hidden = jnp.dot(pooled_all[view_idx], proj_in, precision=HIGHEST, preferred_element_type=jnp.float32)
        normed, scale = batch_norm(hidden)
        gained = normed * proj_gain
        relu_b = jnp.maximum(gained, 0.0).astype(jnp.bfloat16)
        z_full = jnp.dot(relu_b, proj_out, preferred_element_type=jnp.float32)
        z_normed, z_scale = batch_norm(z_full)
        hidden_x.append(normed)
        hidden_s.append(scale)
        hidden_n.append(gained)
        z_x.append(z_normed)
        z_s.append(z_scale)
        z_n.append(z_normed.astype(jnp.bfloat16))
    corr = jnp.dot(z_n[0].T, z_n[1], preferred_element_type=jnp.float32) / clip_total
    eye_mask = jnp.arange(corr.shape[0])[:, None] == jnp.arange(corr.shape[1])[None, :]
    dcorr = jnp.where(eye_mask, -2.0 * (1.0 - corr), 2.0 * LAMBDA_OFF * corr)
    zn_rgb = z_n[0].astype(jnp.float32)
    zn_flow = z_n[1].astype(jnp.float32)
    dzn = [jnp.dot(zn_flow, dcorr.T, precision=HIGHEST) / clip_total, jnp.dot(zn_rgb, dcorr, precision=HIGHEST) / clip_total]
    dpooled = []
    for view_idx in range(2):
        grad_zn = dzn[view_idx]
        dz_b = ((grad_zn - lax.optimization_barrier(jnp.mean(grad_zn, axis=0)) - z_x[view_idx] * lax.optimization_barrier(jnp.mean(grad_zn * z_x[view_idx], axis=0))) * z_s[view_idx]).astype(jnp.bfloat16)
        drelu = jnp.dot(dz_b, proj_out.T, preferred_element_type=jnp.float32)
        dxh = jnp.where(hidden_n[view_idx] > 0, drelu, 0.0) * proj_gain
        xh_now = hidden_x[view_idx]
        dhidden = (dxh - lax.optimization_barrier(jnp.mean(dxh, axis=0)) - xh_now * lax.optimization_barrier(jnp.mean(dxh * xh_now, axis=0))) * hidden_s[view_idx]
        dpooled.append(jnp.dot(dhidden, proj_in.T, precision=HIGHEST))
    grads_in, grads_out = ([], [])
    for view_idx in range(2):
        in_w = in_weights[view_idx]
        out_w = out_weights[view_idx]
        decays = decay[view_idx]
        skip_v = skip[view_idx]
        decay_next = jnp.concatenate([decays[1:], jnp.zeros((1, decays.shape[1]), jnp.float32)], axis=0)

        def clip_grads(totals, pair_in, in_w=in_w, out_w=out_w, decays=decays, skip_v=skip_v, decay_next=decay_next):
            clip_maps, dpool = pair_in
            inputs, states_b, mixed_out = view_forward(clip_maps, in_w, out_w, decays, skip_v)
            dmix = dpool / cell_count * silu_grad(mixed_out)
            dmix_b = dmix.astype(jnp.bfloat16)
            out_grad = weight_product(states_b, dmix_b)
            from_out = convolve(dmix_b, flipped(out_w), -1)

            def retreat(carried, pair_back):
                decay_after, source = pair_back
                carried = source + decay_after * carried
                return (carried, carried)
            _, adjoint = lax.scan(retreat, jnp.zeros(clip_maps.shape[1:], jnp.float32), (decay_next, from_out), reverse=True)
            dinput = (adjoint + skip_v * dmix).astype(jnp.bfloat16)
            in_grad = weight_product(clip_maps, dinput)
            return ((totals[0] + in_grad, totals[1] + out_grad), None)
        zero_grad = jnp.zeros(in_w.shape, jnp.float32)
        (in_total, out_total), _ = lax.scan(clip_grads, (zero_grad, zero_grad), (views[view_idx], dpooled[view_idx]))
        grads_in.append(in_total)
        grads_out.append(out_total)
    return (jnp.stack(grads_in), jnp.stack(grads_out))
```

```python
import functools

import jax
import jax.numpy as jnp
from jax import lax
from jax.experimental import pallas as pl
from jax.experimental.pallas import tpu as pltpu
from jax.sharding import PartitionSpec as P

LAMBDA_OFF = 0.0051
EPSILON = 1e-05
HIGHEST = lax.Precision.HIGHEST


def prefix(x, axis, combine, identity, reverse):
    peers, here = (lax.axis_size(axis), lax.axis_index(axis))
    everything = jax.tree.map(lambda part: lax.all_gather(part, axis), x)
    start = jax.tree.map(
        lambda part, zero: jnp.broadcast_to(jnp.asarray(zero, part.dtype), part.shape), x, identity
    )

    def lap(k, before):
        at = peers - 1 - k if reverse else k
        reached = at > here if reverse else at < here
        new = combine(before, jax.tree.map(lambda part: part[at], everything))
        return jax.tree.map(lambda a, b: jnp.where(reached, a, b), new, before)

    return lax.fori_loop(0, peers, lap, start)


def patches(feature_maps, flip_sign):
    map_side = feature_maps.shape[-2]
    padding = [(0, 0)] * (feature_maps.ndim - 3) + [(1, 1), (1, 1), (0, 0)]
    padded = jnp.pad(feature_maps, padding)
    pieces = []
    for row_off in range(3):
        for col_off in range(3):
            top_row = 1 + flip_sign * (row_off - 1)
            left_col = 1 + flip_sign * (col_off - 1)
            pieces.append(
                padded[..., top_row : top_row + map_side, left_col : left_col + map_side, :]
            )
    return jnp.concatenate(pieces, axis=-1)


def convolve(feature_maps, weights, flip_sign):
    stacked = patches(feature_maps, flip_sign)
    flat = stacked.reshape(-1, stacked.shape[-1])
    result = jnp.dot(flat, weights, preferred_element_type=jnp.float32)
    return result.reshape(feature_maps.shape[:-1] + (weights.shape[1],))


def flipped(weights):
    channels = weights.shape[1]
    return weights.reshape(9, channels, channels).transpose(0, 2, 1).reshape(9 * channels, channels)


def weight_product(feature_maps, grads):
    stacked = patches(feature_maps, 1)
    flat = stacked.reshape(-1, stacked.shape[-1])
    return lax.dot_general(
        flat,
        grads.reshape(-1, grads.shape[-1]),
        (((0,), (0,)), ((), ())),
        preferred_element_type=jnp.float32,
    )


def silu_grad(values):
    sigma = jax.nn.sigmoid(values)
    return sigma * (1.0 + values * (1.0 - sigma))


def compose(earlier, latter):
    return (earlier[0] * latter[0], latter[0] * earlier[1] + latter[1])


def compose_pair(earlier, latter):
    first_view = compose((earlier[0], earlier[1]), (latter[0], latter[1]))
    second_view = compose((earlier[2], earlier[3]), (latter[2], latter[3]))
    return (first_view[0], first_view[1], second_view[0], second_view[1])


def local_states(view_maps, in_w, decays):
    inputs = convolve(view_maps, in_w, 1).astype(jnp.bfloat16)
    frames_here = view_maps.shape[1]
    carried = jnp.zeros(view_maps.shape[:1] + view_maps.shape[2:], jnp.float32)
    collected = []
    for frame_idx in range(frames_here):
        carried = decays[frame_idx] * carried + inputs[:, frame_idx].astype(jnp.float32)
        collected.append(carried)
    return (inputs, jnp.stack(collected, axis=1), jnp.prod(decays, axis=0), carried)


def finish_states(inputs, partial_states, decays, incoming, out_w, skip_v):
    running = jnp.cumprod(decays, axis=0)
    states = partial_states + running[None, :, None, None, :] * incoming[:, None]
    states_b = states.astype(jnp.bfloat16)
    mixed_out = convolve(states_b, out_w, 1) + skip_v * inputs.astype(jnp.float32)
    pooled_part = jnp.sum(jax.nn.silu(mixed_out), axis=(1, 2, 3))
    return (states_b, mixed_out, pooled_part)


def local_adjoint(dpool, mixed_out, states_b, decays, out_w, cell_count):
    dmix = dpool[:, None, None, None, :] / cell_count * silu_grad(mixed_out)
    dmix_b = dmix.astype(jnp.bfloat16)
    out_grad = weight_product(states_b, dmix_b)
    from_out = convolve(dmix_b, flipped(out_w), -1)
    frames_here = mixed_out.shape[1]
    adjoint_list = [None] * frames_here
    carried = from_out[:, frames_here - 1]
    adjoint_list[frames_here - 1] = carried
    for frame_idx in range(frames_here - 2, -1, -1):
        carried = from_out[:, frame_idx] + decays[frame_idx + 1] * carried
        adjoint_list[frame_idx] = carried
    partial_adjoint = jnp.stack(adjoint_list, axis=1)
    return (dmix, out_grad, partial_adjoint, decays[0] * partial_adjoint[:, 0])


def finish_adjoint(view_maps, dmix, partial_adjoint, decays, incoming, skip_v):
    reversed_prod = jnp.cumprod(decays[::-1], axis=0)[::-1]
    after_prod = jnp.concatenate(
        [reversed_prod[1:], jnp.ones((1, decays.shape[1]), jnp.float32)], axis=0
    )
    adjoint = partial_adjoint + after_prod[None, :, None, None, :] * incoming[:, None]
    dinput = (adjoint + skip_v * dmix).astype(jnp.bfloat16)
    return weight_product(view_maps, dinput)


def barlow_grads(corr_rows, first_row):
    row_ids = jnp.arange(corr_rows.shape[0]) + first_row
    eye_mask = row_ids[:, None] == jnp.arange(corr_rows.shape[1])[None, :]
    return jnp.where(eye_mask, -2.0 * (1.0 - corr_rows), 2.0 * LAMBDA_OFF * corr_rows)


def scanned_per_device(
    rgb_maps, flow_maps, in_weights, out_weights, decay, skip, proj_in, proj_gain, proj_out
):
    channels = rgb_maps.shape[-1]
    state_shape = rgb_maps.shape[:1] + rgb_maps.shape[2:]
    unit_decay = jnp.ones((channels,), jnp.float32)
    zero_state = jnp.zeros(state_shape, jnp.float32)
    cell_count = rgb_maps.shape[1] * lax.axis_size("tm") * rgb_maps.shape[2] * rgb_maps.shape[3]
    clip_total = rgb_maps.shape[0] * lax.axis_size("batch")
    in_rgb, part_rgb, total_rgb, end_rgb = local_states(rgb_maps, in_weights[0], decay[0])
    in_flow, part_flow, total_flow, end_flow = local_states(flow_maps, in_weights[1], decay[1])
    scanned = prefix(
        (total_rgb, end_rgb, total_flow, end_flow),
        "tm",
        compose_pair,
        (unit_decay, zero_state, unit_decay, zero_state),
        False,
    )
    income_rgb = scanned[1]
    income_flow = scanned[3]
    states_rgb, mixed_rgb, pooled_rgb = finish_states(
        in_rgb, part_rgb, decay[0], income_rgb, out_weights[0], skip[0]
    )
    states_flow, mixed_flow, pooled_flow = finish_states(
        in_flow, part_flow, decay[1], income_flow, out_weights[1], skip[1]
    )
    pooled_sums = lax.psum((pooled_rgb, pooled_flow), "tm")
    pooled_views = (pooled_sums[0] / cell_count, pooled_sums[1] / cell_count)
    hidden_views = [
        jnp.dot(
            pooled_views[view_idx], proj_in, precision=HIGHEST, preferred_element_type=jnp.float32
        )
        for view_idx in range(2)
    ]
    hidden_totals = lax.psum(
        (jnp.sum(hidden_views[0], axis=0), jnp.sum(hidden_views[1], axis=0)), "batch"
    )
    hidden_cent = [
        hidden_views[view_idx] - hidden_totals[view_idx] / clip_total for view_idx in range(2)
    ]
    hidden_squares = lax.psum(
        (
            jnp.sum(hidden_cent[0] * hidden_cent[0], axis=0),
            jnp.sum(hidden_cent[1] * hidden_cent[1], axis=0),
        ),
        "batch",
    )
    hidden_scale = [
        lax.rsqrt(hidden_squares[view_idx] / clip_total + EPSILON) for view_idx in range(2)
    ]
    hidden_x = [hidden_cent[view_idx] * hidden_scale[view_idx] for view_idx in range(2)]
    hidden_n = [hidden_x[view_idx] * proj_gain for view_idx in range(2)]
    z_views = [
        jnp.dot(
            jnp.maximum(hidden_n[view_idx], 0.0).astype(jnp.bfloat16),
            proj_out,
            preferred_element_type=jnp.float32,
        )
        for view_idx in range(2)
    ]
    z_totals = lax.psum((jnp.sum(z_views[0], axis=0), jnp.sum(z_views[1], axis=0)), "batch")
    z_cent = [z_views[view_idx] - z_totals[view_idx] / clip_total for view_idx in range(2)]
    z_squares = lax.psum(
        (jnp.sum(z_cent[0] * z_cent[0], axis=0), jnp.sum(z_cent[1] * z_cent[1], axis=0)), "batch"
    )
    z_scale = [lax.rsqrt(z_squares[view_idx] / clip_total + EPSILON) for view_idx in range(2)]
    z_x = [z_cent[view_idx] * z_scale[view_idx] for view_idx in range(2)]
    zn_rgb = z_x[0].astype(jnp.bfloat16)
    zn_flow = z_x[1].astype(jnp.bfloat16)
    proj_width = proj_out.shape[1]
    row_block = proj_width // lax.axis_size("tm")
    first_row = lax.axis_index("tm") * row_block
    own_block = lax.dynamic_slice_in_dim(zn_rgb, first_row, row_block, 1)
    gathered_block, gathered_flow = (
        lax.all_gather(own_block, "batch", axis=0, tiled=True),
        lax.all_gather(zn_flow, "batch", axis=0, tiled=True),
    )
    corr_block = (
        lax.dot_general(
            gathered_block,
            gathered_flow,
            (((0,), (0,)), ((), ())),
            preferred_element_type=jnp.float32,
        )
        / clip_total
    )
    grad_block = barlow_grads(corr_block, first_row)
    flow_wide = zn_flow.astype(jnp.float32)
    block_wide = own_block.astype(jnp.float32)
    dzn_cols = (
        lax.dot_general(flow_wide, grad_block, (((1,), (1,)), ((), ())), precision=HIGHEST)
        / clip_total
    )
    dzn_rgb = lax.all_gather(dzn_cols, "tm", axis=1, tiled=True)
    dzn_flow = lax.psum(jnp.dot(block_wide, grad_block, precision=HIGHEST) / clip_total, "tm")
    dzn_views = (dzn_rgb, dzn_flow)
    z_back = lax.psum(
        (
            jnp.sum(dzn_rgb, axis=0),
            jnp.sum(dzn_rgb * z_x[0], axis=0),
            jnp.sum(dzn_flow, axis=0),
            jnp.sum(dzn_flow * z_x[1], axis=0),
        ),
        "batch",
    )
    dxh_views = []
    for view_idx in range(2):
        dz_b = (
            (
                dzn_views[view_idx]
                - z_back[2 * view_idx] / clip_total
                - z_x[view_idx] * (z_back[2 * view_idx + 1] / clip_total)
            )
            * z_scale[view_idx]
        ).astype(jnp.bfloat16)
        drelu = lax.dot_general(
            dz_b, proj_out, (((1,), (1,)), ((), ())), preferred_element_type=jnp.float32
        )
        dxh_views.append(jnp.where(hidden_n[view_idx] > 0, drelu, 0.0) * proj_gain)
    h_back = lax.psum(
        (
            jnp.sum(dxh_views[0], axis=0),
            jnp.sum(dxh_views[0] * hidden_x[0], axis=0),
            jnp.sum(dxh_views[1], axis=0),
            jnp.sum(dxh_views[1] * hidden_x[1], axis=0),
        ),
        "batch",
    )
    dpooled = []
    for view_idx in range(2):
        dhidden = (
            dxh_views[view_idx]
            - h_back[2 * view_idx] / clip_total
            - hidden_x[view_idx] * (h_back[2 * view_idx + 1] / clip_total)
        ) * hidden_scale[view_idx]
        dpooled.append(
            lax.dot_general(dhidden, proj_in, (((1,), (1,)), ((), ())), precision=HIGHEST)
        )
    dmix_rgb, out_grad_rgb, adj_rgb, send_rgb = local_adjoint(
        dpooled[0], mixed_rgb, states_rgb, decay[0], out_weights[0], cell_count
    )
    dmix_flow, out_grad_flow, adj_flow, send_flow = local_adjoint(
        dpooled[1], mixed_flow, states_flow, decay[1], out_weights[1], cell_count
    )
    returned = prefix(
        (total_rgb, send_rgb, total_flow, send_flow),
        "tm",
        compose_pair,
        (unit_decay, zero_state, unit_decay, zero_state),
        True,
    )
    back_rgb = returned[1]
    back_flow = returned[3]
    in_grad_rgb = finish_adjoint(rgb_maps, dmix_rgb, adj_rgb, decay[0], back_rgb, skip[0])
    in_grad_flow = finish_adjoint(flow_maps, dmix_flow, adj_flow, decay[1], back_flow, skip[1])
    in_stack = jnp.stack([in_grad_rgb, in_grad_flow])
    out_stack = jnp.stack([out_grad_rgb, out_grad_flow])
    shares = (
        lax.psum_scatter(in_stack, "tm", scatter_dimension=1, tiled=True),
        lax.psum_scatter(out_stack, "tm", scatter_dimension=1, tiled=True),
    )
    share_sums = lax.psum((shares[0], shares[1]), "batch")
    whole = (
        lax.all_gather(share_sums[0], "tm", axis=1, tiled=True),
        lax.all_gather(share_sums[1], "tm", axis=1, tiled=True),
    )
    return (whole[0], whole[1])


BLOCK = 8
VMEM_BYTES = 56 * 1024 * 1024


MESH = pl.DeviceIdType.MESH


def greet(places):
    barrier = pltpu.get_barrier_semaphore()
    for place in places:
        pl.semaphore_signal(barrier, inc=1, device_id=place, device_id_type=MESH)
    pl.semaphore_wait(barrier, len(places))


def exchange_kernel(rgb, flow, decay, maps, decays, send, recv, send_decay, recv_decay, own):
    me, peers = (lax.axis_index("tm"), lax.axis_size("tm"))
    clips, frames = rgb.shape[:2]
    here = pl.ds(pl.multiple_of(me * frames, frames), frames)
    others = [lax.rem(me + k, peers) for k in range(1, peers)]
    greet([{"tm": other} for other in others])
    for view, source in enumerate((rgb, flow)):

        @pl.when(me // clips == view)
        def _(source=source):
            pltpu.make_async_copy(source.at[lax.rem(me, clips)], maps.at[here], own.at[0]).start()

    kept = pltpu.make_async_copy(decay.at[me // clips], decays.at[here], own.at[1])
    kept.start()
    copies = []
    for k, other in enumerate(others):
        for view, source in enumerate((rgb, flow)):
            copy = pltpu.make_async_remote_copy(
                src_ref=source.at[lax.rem(other, clips)],
                dst_ref=maps.at[here],
                send_sem=send.at[k],
                recv_sem=recv.at[k],
                device_id={"tm": other},
                device_id_type=MESH,
            )

            @pl.when(other // clips == view)
            def _(copy=copy):
                copy.start()

        copies.append(copy)
        small = pltpu.make_async_remote_copy(
            src_ref=decay.at[other // clips],
            dst_ref=decays.at[here],
            send_sem=send_decay.at[k],
            recv_sem=recv_decay.at[k],
            device_id={"tm": other},
            device_id_type=MESH,
        )
        small.start()
        copies.append(small)
    for copy in copies:
        copy.wait()
    pltpu.make_async_copy(rgb.at[0], maps.at[here], own.at[0]).wait()
    kept.wait()


def exchange(rgb_maps, flow_maps, decay):
    clips, frames = rgb_maps.shape[:2]
    peers = lax.axis_size("tm")
    channels = decay.shape[-1]
    others = pltpu.SemaphoreType.DMA((peers - 1,))
    return pl.pallas_call(
        exchange_kernel,
        in_specs=[pl.BlockSpec(memory_space=pl.ANY)] * 3,
        out_specs=[pl.BlockSpec(memory_space=pl.ANY)] * 2,
        out_shape=[
            jax.ShapeDtypeStruct((frames * peers,) + rgb_maps.shape[2:], rgb_maps.dtype),
            jax.ShapeDtypeStruct((frames * peers, channels), decay.dtype),
        ],
        scratch_shapes=[others, others, others, others, pltpu.SemaphoreType.DMA((2,))],
        compiler_params=pltpu.CompilerParams(collective_id=0, has_side_effects=True),
    )(rgb_maps, flow_maps, decay)


def gather_kernel(pooled, everyone, send, recv):
    me, peers = (lax.axis_index("tm"), lax.axis_size("tm"))
    ring, rings = (lax.axis_index("batch"), lax.axis_size("batch"))
    near = [{"tm": lax.rem(me + k, peers)} for k in range(1, peers)]
    far = [{"batch": lax.rem(ring + k, rings)} for k in range(1, rings)]
    greet(near + far)
    everyone[ring, me] = pooled[...]
    copies = []
    for wave, part in ((near, everyone.at[ring, me]), (far, everyone.at[ring])):
        started = []
        for place in wave:
            at = len(copies) + len(started)
            copy = pltpu.make_async_remote_copy(
                src_ref=part,
                dst_ref=part,
                send_sem=send.at[at],
                recv_sem=recv.at[at],
                device_id=place,
                device_id_type=MESH,
            )
            copy.start()
            started.append(copy)
        for copy in started:
            copy.wait_recv()
        copies += started
    for copy in copies:
        copy.wait_send()


def gather(pooled):
    peers, rings = (lax.axis_size("tm"), lax.axis_size("batch"))
    count = pltpu.SemaphoreType.DMA((peers + rings - 2,))
    return pl.pallas_call(
        gather_kernel,
        in_specs=[pl.BlockSpec(memory_space=pltpu.VMEM)],
        out_specs=pl.BlockSpec(memory_space=pltpu.VMEM),
        out_shape=jax.ShapeDtypeStruct((rings, peers) + pooled.shape, pooled.dtype),
        scratch_shapes=[count, count],
        compiler_params=pltpu.CompilerParams(collective_id=1, has_side_effects=True),
    )(pooled)


def reduce_kernel(grads, whole, from_core, to_x, from_x, acc, from_ring, send, recv):
    me, ring, rings = (lax.axis_index("tm"), lax.axis_index("batch"), lax.axis_size("batch"))
    core, x, y = (lax.rem(me, 2), lax.rem(me // 2, 2), me // 4)
    sibling, across, beyond = (
        {"tm": me + 1 - 2 * core},
        {"tm": me + 2 - 4 * x},
        {"tm": me + 4 - 8 * y},
    )
    others = [lax.rem(ring + k, rings) for k in range(1, rings)]
    greet([sibling, across, beyond] + [{"batch": other} for other in others])
    started = []

    def push(source, target, place):
        at = len(started)
        copy = pltpu.make_async_remote_copy(
            src_ref=source,
            dst_ref=target,
            send_sem=send.at[at],
            recv_sem=recv.at[at],
            device_id=place,
            device_id_type=MESH,
        )
        copy.start()
        started.append(copy)
        return copy

    passed = push(grads.at[1 - core, 1 - x], from_core.at[0], sibling)
    kept = push(grads.at[1 - core, x], from_core.at[1], sibling)
    passed.wait_recv()
    to_x[...] = grads[core, 1 - x] + from_core[0]
    crossed = push(to_x, from_x, across)
    kept.wait_recv()
    acc[...] = grads[core, x] + from_core[1]
    crossed.wait_recv()
    acc[...] += from_x[...]
    arrivals = [
        push(acc.at[other], from_ring.at[k], {"batch": other}) for k, other in enumerate(others)
    ]
    total = acc[ring]
    for k, copy in enumerate(arrivals):
        copy.wait_recv()
        total = total + from_ring[k]
    whole[y, core, x, ring] = total.astype(whole.dtype)
    part = whole.at[y, core, x, ring]
    for copy in [push(part, part, {"batch": other}) for other in others]:
        copy.wait_recv()

    def hand(at_y, at_x, place):
        part = whole.at[at_y, core, at_x]
        return push(part, part, place)

    sideways, upward, inward = (hand(y, x, across), hand(y, x, beyond), [hand(y, x, sibling)])
    sideways.wait_recv()
    corner = hand(y, 1 - x, beyond)
    inward.append(hand(y, 1 - x, sibling))
    upward.wait_recv()
    inward.append(hand(1 - y, x, sibling))
    corner.wait_recv()
    inward.append(hand(1 - y, 1 - x, sibling))
    for copy in inward:
        copy.wait_recv()
    for copy in started:
        copy.wait_send()


def reduce_grads(grads):
    rings = lax.axis_size("batch")
    rows, channels = grads.shape
    part = (rings, rows // (4 * rings), channels)
    count = pltpu.SemaphoreType.DMA((3 + 2 * (rings - 1) + 7,))
    return pl.pallas_call(
        reduce_kernel,
        in_specs=[pl.BlockSpec(memory_space=pltpu.VMEM)],
        out_specs=pl.BlockSpec(memory_space=pltpu.VMEM),
        out_shape=jax.ShapeDtypeStruct((2, 2, 2) + part, jnp.bfloat16),
        scratch_shapes=[
            pltpu.VMEM((2,) + part, jnp.float32),
            pltpu.VMEM(part, jnp.float32),
            pltpu.VMEM(part, jnp.float32),
            pltpu.VMEM(part, jnp.float32),
            pltpu.VMEM((rings - 1,) + part[1:], jnp.float32),
            count,
            count,
        ],
        compiler_params=pltpu.CompilerParams(
            collective_id=2, has_side_effects=True, vmem_limit_bytes=VMEM_BYTES
        ),
    )(grads.reshape((2, 2) + part))


def pair_weights(weights):
    channels = weights.shape[1]
    by_row = weights.reshape(3, 3 * channels, channels)
    none = jnp.zeros((1, 3 * channels, channels), weights.dtype)
    upper = jnp.concatenate([by_row, none], axis=0)
    lower = jnp.concatenate([none, by_row], axis=0)
    return jnp.concatenate([upper, lower], axis=-1).reshape(12 * channels, 2 * channels)


def transposed(weights):
    channels = weights.shape[1]
    taps = weights.reshape(9, channels, channels)[::-1].transpose(0, 2, 1)
    return taps.reshape(9 * channels, channels)


def column_shifts(values):
    shape = values.shape
    side, channels = shape[-2], shape[-1]
    flat = values.reshape(-1, channels)
    rows = flat.shape[0]
    column = lax.rem(lax.broadcasted_iota(jnp.int32, flat.shape, 0), side)
    left = jnp.where(column == 0, 0.0, pltpu.roll(flat, 1, 0))
    right = jnp.where(column == side - 1, 0.0, pltpu.roll(flat, rows - 1, 0))
    return [part.astype(jnp.bfloat16).reshape(shape) for part in (left, flat, right)]


def put_shifts(padded, values):
    channels = values.shape[-1]
    half = values.shape[1]
    for at, part in enumerate(column_shifts(values)):
        lanes = slice(at * channels, (at + 1) * channels)
        padded[:, 0:half, 1, :, lanes] = part[:, :, 0]
        padded[:, 1 : half + 1, 0, :, lanes] = part[:, :, 1]


def conv_rows(padded, weights):
    half = padded.shape[1] - 1
    stacked = jnp.concatenate(
        [padded[:, 0:half, 0], padded[:, 0:half, 1], padded[:, 1:, 0], padded[:, 1:, 1]], axis=-1
    )
    lead = stacked.shape[:-1]
    out = jnp.dot(
        stacked.reshape(-1, stacked.shape[-1]), weights, preferred_element_type=jnp.float32
    )
    channels = weights.shape[1] // 2
    return (
        out[:, :channels].reshape(lead + (channels,)),
        out[:, channels:].reshape(lead + (channels,)),
    )


def clear_edges(padded):
    shape = padded.shape
    none = jnp.zeros((shape[0],) + shape[3:], padded.dtype)
    padded[:, 0, 0] = none
    padded[:, shape[1] - 1, 1] = none


def forward_kernel(
    maps, in_w, out_w, decay, skip, inputs, states_b, mixed, pooled, padded, states, carried
):
    step = pl.program_id(0)

    @pl.when(step == 0)
    def _():
        clear_edges(padded)
        carried[...] = jnp.zeros_like(carried)
        pooled[...] = jnp.zeros_like(pooled)

    put_shifts(padded, maps[...].astype(jnp.float32))
    even, odd = conv_rows(padded, in_w[...])
    inputs[:, :, 0] = even.astype(jnp.bfloat16)
    inputs[:, :, 1] = odd.astype(jnp.bfloat16)
    for frame in range(maps.shape[0]):
        now = decay[frame : frame + 1, :].reshape(1, 1, 1, -1)
        state = now * carried[...] + inputs[frame].astype(jnp.float32)
        carried[...] = state
        states[frame] = state
        states_b[frame] = state.astype(jnp.bfloat16)
    put_shifts(padded, states_b[...].astype(jnp.float32))
    gain = skip[...].reshape(1, 1, 1, -1)
    total = pooled[...]
    for parity, out in enumerate(conv_rows(padded, out_w[...])):
        value = out + gain * inputs[:, :, parity].astype(jnp.float32)
        mixed[:, :, parity] = value
        active = value * jax.nn.sigmoid(value)
        total = total + jnp.sum(active.reshape(-1, 8, active.shape[-1]), axis=0)
    pooled[...] = total


def put_rows(rows, values):
    frames, half, _, side, channels = values.shape
    rows[:, 1 : 2 * half + 1] = values.reshape(frames, 2 * half, side, channels)


def tap_product(rows, padded):
    height = rows.shape[1] - 2
    left = jnp.concatenate([rows[:, k : k + height] for k in range(3)], axis=-1)
    frames, half = padded.shape[0], padded.shape[1] - 1
    right = padded[...].reshape(frames, 2 * half + 2, padded.shape[3], padded.shape[4])
    right = right[:, 1 : 2 * half + 1]
    return lax.dot_general(
        left.reshape(-1, left.shape[-1]),
        right.reshape(-1, right.shape[-1]),
        (((0,), (0,)), ((), ())),
        preferred_element_type=jnp.float32,
    )


def backward_kernel(
    maps, states_b, mixed, dpool, back_w, after, skip, grads, padded, rows, dmix, total, carried
):
    step = pl.program_id(0)

    @pl.when(step == 0)
    def _():
        clear_edges(padded)
        rows[:, 0] = jnp.zeros_like(rows[:, 0])
        rows[:, rows.shape[1] - 1] = jnp.zeros_like(rows[:, 0])
        carried[...] = jnp.zeros_like(carried)
        total[...] = jnp.zeros_like(total)

    value = mixed[...]
    sigma = jax.nn.sigmoid(value)
    slope = dpool[...].reshape(1, 1, 1, 1, -1)
    dmix[...] = slope * (sigma * (1.0 + value * (1.0 - sigma)))
    put_shifts(padded, dmix[...].astype(jnp.bfloat16).astype(jnp.float32))
    put_rows(rows, states_b[...])
    total[1] += tap_product(rows, padded)
    even, odd = conv_rows(padded, back_w[...])
    gain = skip[...].reshape(1, 1, 1, -1)
    for frame in reversed(range(maps.shape[0])):
        now = after[frame : frame + 1, :].reshape(1, 1, -1)
        for parity, out in enumerate((even, odd)):
            adjoint = out[frame] + now * carried[:, parity]
            carried[:, parity] = adjoint
            dmix[frame, :, parity] = adjoint + gain[0] * dmix[frame, :, parity]
    put_shifts(padded, dmix[...].astype(jnp.bfloat16).astype(jnp.float32))
    put_rows(rows, maps[...])
    total[0] += tap_product(rows, padded)

    @pl.when(step == pl.num_programs(0) - 1)
    def _():
        channels = skip.shape[1]
        for which in range(2):
            for row in range(3):
                for col in range(3):
                    tap = 3 * row + col
                    grads[which, tap * channels : (tap + 1) * channels, :] = total[
                        which,
                        row * channels : (row + 1) * channels,
                        (2 - col) * channels : (3 - col) * channels,
                    ]


def middle_kernel(pooled, proj_in, gain, proj_out, dpooled):
    clips = pooled.shape[0] // 2
    hidden = jnp.dot(
        pooled[...], proj_in[...], precision=HIGHEST, preferred_element_type=jnp.float32
    )

    def mean(values):
        return jnp.sum(values, axis=0, keepdims=True) / clips

    def normed(values):
        centered = values - mean(values)
        scale = lax.rsqrt(mean(centered * centered) + EPSILON)
        return (centered * scale, scale)

    def backed(grad, values, scale):
        return (grad - mean(grad) - values * mean(grad * values)) * scale

    gains = gain[...]
    hidden_x, hidden_s, hidden_n = ([], [], [])
    for view in range(2):
        values, scale = normed(hidden[view * clips : (view + 1) * clips])
        hidden_x.append(values)
        hidden_s.append(scale)
        hidden_n.append(values * gains)
    relu_b = jnp.concatenate([jnp.maximum(part, 0.0) for part in hidden_n], axis=0)
    z_both = jnp.dot(
        relu_b.astype(jnp.bfloat16), proj_out[...], preferred_element_type=jnp.float32
    )
    z_x, z_s, z_n = ([], [], [])
    for view in range(2):
        values, scale = normed(z_both[view * clips : (view + 1) * clips])
        z_x.append(values)
        z_s.append(scale)
        z_n.append(values.astype(jnp.bfloat16).astype(jnp.float32))
    agree = mean(z_n[0] * z_n[1])
    extra = -2.0 * (1.0 - agree) - 2.0 * LAMBDA_OFF * agree
    dz = []
    for view in range(2):
        mine, other = z_n[view], z_n[1 - view]
        other_b = other.astype(jnp.bfloat16)
        gram = lax.dot_general(
            other_b, other_b, (((1,), (1,)), ((), ())), preferred_element_type=jnp.float32
        )
        spread = jnp.dot(
            gram * (2.0 * LAMBDA_OFF / clips),
            mine,
            precision=HIGHEST,
            preferred_element_type=jnp.float32,
        )
        dzn = (spread + other * extra) / clips
        dz.append(backed(dzn, z_x[view], z_s[view]))
    drelu = lax.dot_general(
        jnp.concatenate(dz, axis=0).astype(jnp.bfloat16),
        proj_out[...],
        (((1,), (1,)), ((), ())),
        preferred_element_type=jnp.float32,
    )
    dhidden = []
    for view in range(2):
        part = drelu[view * clips : (view + 1) * clips]
        dxh = jnp.where(hidden_n[view] > 0, part, 0.0) * gains
        dhidden.append(backed(dxh, hidden_x[view], hidden_s[view]))
    dpooled[...] = lax.dot_general(
        jnp.concatenate(dhidden, axis=0),
        proj_in[...],
        (((1,), (1,)), ((), ())),
        precision=HIGHEST,
        preferred_element_type=jnp.float32,
    )


def forward(maps, in_w, out_w, decay, skip):
    frames, half, _, side, channels = maps.shape
    steps = frames // BLOCK
    shape = (BLOCK, half, 2, side, channels)
    frame_spec = pl.BlockSpec(shape, lambda i: (i, 0, 0, 0, 0))
    whole = pl.BlockSpec(memory_space=pltpu.VMEM)
    return pl.pallas_call(
        forward_kernel,
        grid=(steps,),
        in_specs=[
            frame_spec,
            whole,
            whole,
            pl.BlockSpec((BLOCK, channels), lambda i: (i, 0)),
            whole,
        ],
        out_specs=[frame_spec, frame_spec, frame_spec, whole],
        out_shape=[
            jax.ShapeDtypeStruct(maps.shape, jnp.bfloat16),
            jax.ShapeDtypeStruct(maps.shape, jnp.bfloat16),
            jax.ShapeDtypeStruct(maps.shape, jnp.float32),
            jax.ShapeDtypeStruct((8, channels), jnp.float32),
        ],
        scratch_shapes=[
            pltpu.VMEM((BLOCK, half + 1, 2, side, 3 * channels), jnp.bfloat16),
            pltpu.VMEM(shape, jnp.float32),
            pltpu.VMEM(shape[1:], jnp.float32),
        ],
        compiler_params=pltpu.CompilerParams(vmem_limit_bytes=VMEM_BYTES),
    )(maps, pair_weights(in_w), pair_weights(out_w), decay, skip)


def backward(maps, states_b, mixed, dpool, out_w, decay, skip):
    frames, half, _, side, channels = maps.shape
    steps = frames // BLOCK
    shape = (BLOCK, half, 2, side, channels)
    frame_spec = pl.BlockSpec(shape, lambda i: (steps - 1 - i, 0, 0, 0, 0))
    whole = pl.BlockSpec(memory_space=pltpu.VMEM)
    after = jnp.concatenate([decay[1:], jnp.zeros((1, channels), jnp.float32)], axis=0)
    return pl.pallas_call(
        backward_kernel,
        grid=(steps,),
        in_specs=[
            frame_spec,
            frame_spec,
            frame_spec,
            whole,
            whole,
            pl.BlockSpec((BLOCK, channels), lambda i: (steps - 1 - i, 0)),
            whole,
        ],
        out_specs=whole,
        out_shape=jax.ShapeDtypeStruct((2, 9 * channels, channels), jnp.float32),
        scratch_shapes=[
            pltpu.VMEM((BLOCK, half + 1, 2, side, 3 * channels), jnp.bfloat16),
            pltpu.VMEM((BLOCK, 2 * half + 2, side, channels), jnp.bfloat16),
            pltpu.VMEM(shape, jnp.float32),
            pltpu.VMEM((2, 3 * channels, 3 * channels), jnp.float32),
            pltpu.VMEM(shape[1:], jnp.float32),
        ],
        compiler_params=pltpu.CompilerParams(vmem_limit_bytes=VMEM_BYTES),
    )(maps, states_b, mixed, dpool, pair_weights(transposed(out_w)), after, skip)


def middle(pooled, proj_in, proj_gain, proj_out):
    whole = pl.BlockSpec(memory_space=pltpu.VMEM)
    return pl.pallas_call(
        middle_kernel,
        in_specs=[whole] * 4,
        out_specs=whole,
        out_shape=jax.ShapeDtypeStruct(pooled.shape, jnp.float32),
        compiler_params=pltpu.CompilerParams(vmem_limit_bytes=VMEM_BYTES),
    )(pooled, proj_in, proj_gain[None], proj_out)


def clip_per_device(
    rgb_maps, flow_maps, in_weights, out_weights, decay, skip, proj_in, proj_gain, proj_out
):
    clips, frames_here, side, _, channels = rgb_maps.shape
    peers, here = (lax.axis_size("tm"), lax.axis_index("tm"))
    rings, ring = (lax.axis_size("batch"), lax.axis_index("batch"))
    frames = frames_here * peers
    view, clip = (here // clips, here % clips)
    maps, decay_v = exchange(rgb_maps, flow_maps, decay)
    maps = maps.reshape(frames, side // 2, 2, side, channels)

    def own(values):
        return lax.dynamic_index_in_dim(values, view, 0, keepdims=False)

    in_w, out_w, skip_v = (own(in_weights), own(out_weights), own(skip))
    cells = frames * side * side
    _, states_b, mixed, pooled = forward(maps, in_w, out_w, decay_v, skip_v[None])
    gathered = jnp.sum(gather(pooled), axis=2) / cells
    gathered = gathered.reshape(rings, 2, clips, channels).transpose(1, 0, 2, 3)
    dpooled = middle(gathered.reshape(-1, channels), proj_in, proj_gain, proj_out)
    row = (view * rings + ring) * clips + clip
    dpool = lax.dynamic_slice_in_dim(dpooled, row, 1, 0) / cells
    grads = backward(maps, states_b, mixed, dpool, out_w, decay_v, skip_v[None])
    whole = reduce_grads(grads.reshape(-1, channels)).astype(jnp.float32)
    whole = whole.reshape(2, 2, 9 * channels, channels)
    return (whole[:, 0], whole[:, 1])


def per_device(rgb_maps, *others):
    clips, frames_here, side = rgb_maps.shape[:3]
    fits = lax.axis_size("tm") == 2 * clips and side % 2 == 0
    fits = fits and clips == 4 and (9 * rgb_maps.shape[-1]) % (32 * lax.axis_size("batch")) == 0
    fits = fits and (frames_here * lax.axis_size("tm")) % BLOCK == 0
    chosen = clip_per_device if fits else scanned_per_device
    return chosen(rgb_maps, *others)


def solution(mesh):
    return jax.shard_map(
        per_device,
        mesh=mesh,
        in_specs=(
            P("batch", "tm", None, None, None),
            P("batch", "tm", None, None, None),
            P(),
            P(),
            P(None, "tm", None),
            P(),
            P(),
            P(),
            P(),
        ),
        out_specs=(P(), P()),
        check_vma=False,
    )
```

```python
import functools

import jax
import jax.numpy as jnp
from jax import lax
from jax.experimental import pallas as pl
from jax.experimental.pallas import tpu as pltpu
from jax.sharding import PartitionSpec as P

LAMBDA_OFF = 0.0051
EPSILON = 1e-05
HIGHEST = lax.Precision.HIGHEST


def prefix(x, axis, combine, identity, reverse):
    peers, here = (lax.axis_size(axis), lax.axis_index(axis))
    everything = jax.tree.map(lambda part: lax.all_gather(part, axis), x)
    start = jax.tree.map(
        lambda part, zero: jnp.broadcast_to(jnp.asarray(zero, part.dtype), part.shape), x, identity
    )

    def lap(k, before):
        at = peers - 1 - k if reverse else k
        reached = at > here if reverse else at < here
        new = combine(before, jax.tree.map(lambda part: part[at], everything))
        return jax.tree.map(lambda a, b: jnp.where(reached, a, b), new, before)

    return lax.fori_loop(0, peers, lap, start)


def patches(feature_maps, flip_sign):
    map_side = feature_maps.shape[-2]
    padding = [(0, 0)] * (feature_maps.ndim - 3) + [(1, 1), (1, 1), (0, 0)]
    padded = jnp.pad(feature_maps, padding)
    pieces = []
    for row_off in range(3):
        for col_off in range(3):
            top_row = 1 + flip_sign * (row_off - 1)
            left_col = 1 + flip_sign * (col_off - 1)
            pieces.append(
                padded[..., top_row : top_row + map_side, left_col : left_col + map_side, :]
            )
    return jnp.concatenate(pieces, axis=-1)


def convolve(feature_maps, weights, flip_sign):
    stacked = patches(feature_maps, flip_sign)
    flat = stacked.reshape(-1, stacked.shape[-1])
    result = jnp.dot(flat, weights, preferred_element_type=jnp.float32)
    return result.reshape(feature_maps.shape[:-1] + (weights.shape[1],))


def flipped(weights):
    channels = weights.shape[1]
    return weights.reshape(9, channels, channels).transpose(0, 2, 1).reshape(9 * channels, channels)


def weight_product(feature_maps, grads):
    stacked = patches(feature_maps, 1)
    flat = stacked.reshape(-1, stacked.shape[-1])
    return lax.dot_general(
        flat,
        grads.reshape(-1, grads.shape[-1]),
        (((0,), (0,)), ((), ())),
        preferred_element_type=jnp.float32,
    )


def silu_grad(values):
    sigma = jax.nn.sigmoid(values)
    return sigma * (1.0 + values * (1.0 - sigma))


def compose(earlier, latter):
    return (earlier[0] * latter[0], latter[0] * earlier[1] + latter[1])


def compose_pair(earlier, latter):
    first_view = compose((earlier[0], earlier[1]), (latter[0], latter[1]))
    second_view = compose((earlier[2], earlier[3]), (latter[2], latter[3]))
    return (first_view[0], first_view[1], second_view[0], second_view[1])


def local_states(view_maps, in_w, decays):
    inputs = convolve(view_maps, in_w, 1).astype(jnp.bfloat16)
    frames_here = view_maps.shape[1]
    carried = jnp.zeros(view_maps.shape[:1] + view_maps.shape[2:], jnp.float32)
    collected = []
    for frame_idx in range(frames_here):
        carried = decays[frame_idx] * carried + inputs[:, frame_idx].astype(jnp.float32)
        collected.append(carried)
    return (inputs, jnp.stack(collected, axis=1), jnp.prod(decays, axis=0), carried)


def finish_states(inputs, partial_states, decays, incoming, out_w, skip_v):
    running = jnp.cumprod(decays, axis=0)
    states = partial_states + running[None, :, None, None, :] * incoming[:, None]
    states_b = states.astype(jnp.bfloat16)
    mixed_out = convolve(states_b, out_w, 1) + skip_v * inputs.astype(jnp.float32)
    pooled_part = jnp.sum(jax.nn.silu(mixed_out), axis=(1, 2, 3))
    return (states_b, mixed_out, pooled_part)


def local_adjoint(dpool, mixed_out, states_b, decays, out_w, cell_count):
    dmix = dpool[:, None, None, None, :] / cell_count * silu_grad(mixed_out)
    dmix_b = dmix.astype(jnp.bfloat16)
    out_grad = weight_product(states_b, dmix_b)
    from_out = convolve(dmix_b, flipped(out_w), -1)
    frames_here = mixed_out.shape[1]
    adjoint_list = [None] * frames_here
    carried = from_out[:, frames_here - 1]
    adjoint_list[frames_here - 1] = carried
    for frame_idx in range(frames_here - 2, -1, -1):
        carried = from_out[:, frame_idx] + decays[frame_idx + 1] * carried
        adjoint_list[frame_idx] = carried
    partial_adjoint = jnp.stack(adjoint_list, axis=1)
    return (dmix, out_grad, partial_adjoint, decays[0] * partial_adjoint[:, 0])


def finish_adjoint(view_maps, dmix, partial_adjoint, decays, incoming, skip_v):
    reversed_prod = jnp.cumprod(decays[::-1], axis=0)[::-1]
    after_prod = jnp.concatenate(
        [reversed_prod[1:], jnp.ones((1, decays.shape[1]), jnp.float32)], axis=0
    )
    adjoint = partial_adjoint + after_prod[None, :, None, None, :] * incoming[:, None]
    dinput = (adjoint + skip_v * dmix).astype(jnp.bfloat16)
    return weight_product(view_maps, dinput)


def barlow_grads(corr_rows, first_row):
    row_ids = jnp.arange(corr_rows.shape[0]) + first_row
    eye_mask = row_ids[:, None] == jnp.arange(corr_rows.shape[1])[None, :]
    return jnp.where(eye_mask, -2.0 * (1.0 - corr_rows), 2.0 * LAMBDA_OFF * corr_rows)


def scanned_per_device(
    rgb_maps, flow_maps, in_weights, out_weights, decay, skip, proj_in, proj_gain, proj_out
):
    channels = rgb_maps.shape[-1]
    state_shape = rgb_maps.shape[:1] + rgb_maps.shape[2:]
    unit_decay = jnp.ones((channels,), jnp.float32)
    zero_state = jnp.zeros(state_shape, jnp.float32)
    cell_count = rgb_maps.shape[1] * lax.axis_size("tm") * rgb_maps.shape[2] * rgb_maps.shape[3]
    clip_total = rgb_maps.shape[0] * lax.axis_size("batch")
    in_rgb, part_rgb, total_rgb, end_rgb = local_states(rgb_maps, in_weights[0], decay[0])
    in_flow, part_flow, total_flow, end_flow = local_states(flow_maps, in_weights[1], decay[1])
    scanned = prefix(
        (total_rgb, end_rgb, total_flow, end_flow),
        "tm",
        compose_pair,
        (unit_decay, zero_state, unit_decay, zero_state),
        False,
    )
    income_rgb = scanned[1]
    income_flow = scanned[3]
    states_rgb, mixed_rgb, pooled_rgb = finish_states(
        in_rgb, part_rgb, decay[0], income_rgb, out_weights[0], skip[0]
    )
    states_flow, mixed_flow, pooled_flow = finish_states(
        in_flow, part_flow, decay[1], income_flow, out_weights[1], skip[1]
    )
    pooled_sums = lax.psum((pooled_rgb, pooled_flow), "tm")
    pooled_views = (pooled_sums[0] / cell_count, pooled_sums[1] / cell_count)
    hidden_views = [
        jnp.dot(
            pooled_views[view_idx], proj_in, precision=HIGHEST, preferred_element_type=jnp.float32
        )
        for view_idx in range(2)
    ]
    hidden_totals = lax.psum(
        (jnp.sum(hidden_views[0], axis=0), jnp.sum(hidden_views[1], axis=0)), "batch"
    )
    hidden_cent = [
        hidden_views[view_idx] - hidden_totals[view_idx] / clip_total for view_idx in range(2)
    ]
    hidden_squares = lax.psum(
        (
            jnp.sum(hidden_cent[0] * hidden_cent[0], axis=0),
            jnp.sum(hidden_cent[1] * hidden_cent[1], axis=0),
        ),
        "batch",
    )
    hidden_scale = [
        lax.rsqrt(hidden_squares[view_idx] / clip_total + EPSILON) for view_idx in range(2)
    ]
    hidden_x = [hidden_cent[view_idx] * hidden_scale[view_idx] for view_idx in range(2)]
    hidden_n = [hidden_x[view_idx] * proj_gain for view_idx in range(2)]
    z_views = [
        jnp.dot(
            jnp.maximum(hidden_n[view_idx], 0.0).astype(jnp.bfloat16),
            proj_out,
            preferred_element_type=jnp.float32,
        )
        for view_idx in range(2)
    ]
    z_totals = lax.psum((jnp.sum(z_views[0], axis=0), jnp.sum(z_views[1], axis=0)), "batch")
    z_cent = [z_views[view_idx] - z_totals[view_idx] / clip_total for view_idx in range(2)]
    z_squares = lax.psum(
        (jnp.sum(z_cent[0] * z_cent[0], axis=0), jnp.sum(z_cent[1] * z_cent[1], axis=0)), "batch"
    )
    z_scale = [lax.rsqrt(z_squares[view_idx] / clip_total + EPSILON) for view_idx in range(2)]
    z_x = [z_cent[view_idx] * z_scale[view_idx] for view_idx in range(2)]
    zn_rgb = z_x[0].astype(jnp.bfloat16)
    zn_flow = z_x[1].astype(jnp.bfloat16)
    proj_width = proj_out.shape[1]
    row_block = proj_width // lax.axis_size("tm")
    first_row = lax.axis_index("tm") * row_block
    own_block = lax.dynamic_slice_in_dim(zn_rgb, first_row, row_block, 1)
    gathered_block, gathered_flow = (
        lax.all_gather(own_block, "batch", axis=0, tiled=True),
        lax.all_gather(zn_flow, "batch", axis=0, tiled=True),
    )
    corr_block = (
        lax.dot_general(
            gathered_block,
            gathered_flow,
            (((0,), (0,)), ((), ())),
            preferred_element_type=jnp.float32,
        )
        / clip_total
    )
    grad_block = barlow_grads(corr_block, first_row)
    flow_wide = zn_flow.astype(jnp.float32)
    block_wide = own_block.astype(jnp.float32)
    dzn_cols = (
        lax.dot_general(flow_wide, grad_block, (((1,), (1,)), ((), ())), precision=HIGHEST)
        / clip_total
    )
    dzn_rgb = lax.all_gather(dzn_cols, "tm", axis=1, tiled=True)
    dzn_flow = lax.psum(jnp.dot(block_wide, grad_block, precision=HIGHEST) / clip_total, "tm")
    dzn_views = (dzn_rgb, dzn_flow)
    z_back = lax.psum(
        (
            jnp.sum(dzn_rgb, axis=0),
            jnp.sum(dzn_rgb * z_x[0], axis=0),
            jnp.sum(dzn_flow, axis=0),
            jnp.sum(dzn_flow * z_x[1], axis=0),
        ),
        "batch",
    )
    dxh_views = []
    for view_idx in range(2):
        dz_b = (
            (
                dzn_views[view_idx]
                - z_back[2 * view_idx] / clip_total
                - z_x[view_idx] * (z_back[2 * view_idx + 1] / clip_total)
            )
            * z_scale[view_idx]
        ).astype(jnp.bfloat16)
        drelu = lax.dot_general(
            dz_b, proj_out, (((1,), (1,)), ((), ())), preferred_element_type=jnp.float32
        )
        dxh_views.append(jnp.where(hidden_n[view_idx] > 0, drelu, 0.0) * proj_gain)
    h_back = lax.psum(
        (
            jnp.sum(dxh_views[0], axis=0),
            jnp.sum(dxh_views[0] * hidden_x[0], axis=0),
            jnp.sum(dxh_views[1], axis=0),
            jnp.sum(dxh_views[1] * hidden_x[1], axis=0),
        ),
        "batch",
    )
    dpooled = []
    for view_idx in range(2):
        dhidden = (
            dxh_views[view_idx]
            - h_back[2 * view_idx] / clip_total
            - hidden_x[view_idx] * (h_back[2 * view_idx + 1] / clip_total)
        ) * hidden_scale[view_idx]
        dpooled.append(
            lax.dot_general(dhidden, proj_in, (((1,), (1,)), ((), ())), precision=HIGHEST)
        )
    dmix_rgb, out_grad_rgb, adj_rgb, send_rgb = local_adjoint(
        dpooled[0], mixed_rgb, states_rgb, decay[0], out_weights[0], cell_count
    )
    dmix_flow, out_grad_flow, adj_flow, send_flow = local_adjoint(
        dpooled[1], mixed_flow, states_flow, decay[1], out_weights[1], cell_count
    )
    returned = prefix(
        (total_rgb, send_rgb, total_flow, send_flow),
        "tm",
        compose_pair,
        (unit_decay, zero_state, unit_decay, zero_state),
        True,
    )
    back_rgb = returned[1]
    back_flow = returned[3]
    in_grad_rgb = finish_adjoint(rgb_maps, dmix_rgb, adj_rgb, decay[0], back_rgb, skip[0])
    in_grad_flow = finish_adjoint(flow_maps, dmix_flow, adj_flow, decay[1], back_flow, skip[1])
    in_stack = jnp.stack([in_grad_rgb, in_grad_flow])
    out_stack = jnp.stack([out_grad_rgb, out_grad_flow])
    shares = (
        lax.psum_scatter(in_stack, "tm", scatter_dimension=1, tiled=True),
        lax.psum_scatter(out_stack, "tm", scatter_dimension=1, tiled=True),
    )
    share_sums = lax.psum((shares[0], shares[1]), "batch")
    whole = (
        lax.all_gather(share_sums[0], "tm", axis=1, tiled=True),
        lax.all_gather(share_sums[1], "tm", axis=1, tiled=True),
    )
    return (whole[0], whole[1])


BLOCK = 8
VMEM_BYTES = 56 * 1024 * 1024


MESH = pl.DeviceIdType.MESH


def greet(places):
    barrier = pltpu.get_barrier_semaphore()
    for place in places:
        pl.semaphore_signal(barrier, inc=1, device_id=place, device_id_type=MESH)
    pl.semaphore_wait(barrier, len(places))


def exchange_kernel(rgb, flow, decay, maps, decays, send, recv, send_decay, recv_decay, own):
    me, peers = (lax.axis_index("tm"), lax.axis_size("tm"))
    clips, frames = rgb.shape[:2]
    here = pl.ds(pl.multiple_of(me * frames, frames), frames)
    others = [lax.rem(me + k, peers) for k in range(1, peers)]
    greet([{"tm": other} for other in others])
    for view, source in enumerate((rgb, flow)):

        @pl.when(me // clips == view)
        def _(source=source):
            pltpu.make_async_copy(source.at[lax.rem(me, clips)], maps.at[here], own.at[0]).start()

    kept = pltpu.make_async_copy(decay.at[me // clips], decays.at[here], own.at[1])
    kept.start()
    copies = []
    for k, other in enumerate(others):
        for view, source in enumerate((rgb, flow)):
            copy = pltpu.make_async_remote_copy(
                src_ref=source.at[lax.rem(other, clips)],
                dst_ref=maps.at[here],
                send_sem=send.at[k],
                recv_sem=recv.at[k],
                device_id={"tm": other},
                device_id_type=MESH,
            )

            @pl.when(other // clips == view)
            def _(copy=copy):
                copy.start()

        copies.append(copy)
        small = pltpu.make_async_remote_copy(
            src_ref=decay.at[other // clips],
            dst_ref=decays.at[here],
            send_sem=send_decay.at[k],
            recv_sem=recv_decay.at[k],
            device_id={"tm": other},
            device_id_type=MESH,
        )
        small.start()
        copies.append(small)
    for copy in copies:
        copy.wait()
    pltpu.make_async_copy(rgb.at[0], maps.at[here], own.at[0]).wait()
    kept.wait()


def exchange(rgb_maps, flow_maps, decay):
    clips, frames = rgb_maps.shape[:2]
    peers = lax.axis_size("tm")
    channels = decay.shape[-1]
    others = pltpu.SemaphoreType.DMA((peers - 1,))
    return pl.pallas_call(
        exchange_kernel,
        in_specs=[pl.BlockSpec(memory_space=pl.ANY)] * 3,
        out_specs=[pl.BlockSpec(memory_space=pl.ANY)] * 2,
        out_shape=[
            jax.ShapeDtypeStruct((frames * peers,) + rgb_maps.shape[2:], rgb_maps.dtype),
            jax.ShapeDtypeStruct((frames * peers, channels), decay.dtype),
        ],
        scratch_shapes=[others, others, others, others, pltpu.SemaphoreType.DMA((2,))],
        compiler_params=pltpu.CompilerParams(collective_id=0, has_side_effects=True),
    )(rgb_maps, flow_maps, decay)


def gather_kernel(pooled, everyone, send, recv):
    me, peers = (lax.axis_index("tm"), lax.axis_size("tm"))
    ring, rings = (lax.axis_index("batch"), lax.axis_size("batch"))
    near = [{"tm": lax.rem(me + k, peers)} for k in range(1, peers)]
    far = [{"batch": lax.rem(ring + k, rings)} for k in range(1, rings)]
    greet(near + far)
    everyone[ring, me] = pooled[...]
    copies = []
    for wave, part in ((near, everyone.at[ring, me]), (far, everyone.at[ring])):
        started = []
        for place in wave:
            at = len(copies) + len(started)
            copy = pltpu.make_async_remote_copy(
                src_ref=part,
                dst_ref=part,
                send_sem=send.at[at],
                recv_sem=recv.at[at],
                device_id=place,
                device_id_type=MESH,
            )
            copy.start()
            started.append(copy)
        for copy in started:
            copy.wait_recv()
        copies += started
    for copy in copies:
        copy.wait_send()


def gather(pooled):
    peers, rings = (lax.axis_size("tm"), lax.axis_size("batch"))
    count = pltpu.SemaphoreType.DMA((peers + rings - 2,))
    return pl.pallas_call(
        gather_kernel,
        in_specs=[pl.BlockSpec(memory_space=pltpu.VMEM)],
        out_specs=pl.BlockSpec(memory_space=pltpu.VMEM),
        out_shape=jax.ShapeDtypeStruct((rings, peers) + pooled.shape, pooled.dtype),
        scratch_shapes=[count, count],
        compiler_params=pltpu.CompilerParams(collective_id=1, has_side_effects=True),
    )(pooled)


def reduce_kernel(grads, whole, from_core, to_x, from_x, acc, from_ring, send, recv):
    me, ring, rings = (lax.axis_index("tm"), lax.axis_index("batch"), lax.axis_size("batch"))
    core, x, y = (lax.rem(me, 2), lax.rem(me // 2, 2), me // 4)
    sibling, across, beyond = (
        {"tm": me + 1 - 2 * core},
        {"tm": me + 2 - 4 * x},
        {"tm": me + 4 - 8 * y},
    )
    others = [lax.rem(ring + k, rings) for k in range(1, rings)]
    greet([sibling, across, beyond] + [{"batch": other} for other in others])
    started = []

    def push(source, target, place):
        at = len(started)
        copy = pltpu.make_async_remote_copy(
            src_ref=source,
            dst_ref=target,
            send_sem=send.at[at],
            recv_sem=recv.at[at],
            device_id=place,
            device_id_type=MESH,
        )
        copy.start()
        started.append(copy)
        return copy

    passed = push(grads.at[1 - core, 1 - x], from_core.at[0], sibling)
    kept = push(grads.at[1 - core, x], from_core.at[1], sibling)
    passed.wait_recv()
    to_x[...] = grads[core, 1 - x] + from_core[0]
    crossed = push(to_x, from_x, across)
    kept.wait_recv()
    acc[...] = grads[core, x] + from_core[1]
    crossed.wait_recv()
    acc[...] += from_x[...]
    arrivals = [
        push(acc.at[other], from_ring.at[k], {"batch": other}) for k, other in enumerate(others)
    ]
    total = acc[ring]
    for k, copy in enumerate(arrivals):
        copy.wait_recv()
        total = total + from_ring[k]
    whole[y, core, x, ring] = total.astype(whole.dtype)
    part = whole.at[y, core, x, ring]
    for copy in [push(part, part, {"batch": other}) for other in others]:
        copy.wait_recv()

    def hand(at_y, at_x, place):
        part = whole.at[at_y, core, at_x]
        return push(part, part, place)

    sideways, upward, inward = (hand(y, x, across), hand(y, x, beyond), [hand(y, x, sibling)])
    sideways.wait_recv()
    corner = hand(y, 1 - x, beyond)
    inward.append(hand(y, 1 - x, sibling))
    upward.wait_recv()
    inward.append(hand(1 - y, x, sibling))
    corner.wait_recv()
    inward.append(hand(1 - y, 1 - x, sibling))
    for copy in inward:
        copy.wait_recv()
    for copy in started:
        copy.wait_send()


def reduce_grads(grads):
    rings = lax.axis_size("batch")
    rows, channels = grads.shape
    part = (rings, rows // (4 * rings), channels)
    count = pltpu.SemaphoreType.DMA((3 + 2 * (rings - 1) + 7,))
    return pl.pallas_call(
        reduce_kernel,
        in_specs=[pl.BlockSpec(memory_space=pltpu.VMEM)],
        out_specs=pl.BlockSpec(memory_space=pltpu.VMEM),
        out_shape=jax.ShapeDtypeStruct((2, 2, 2) + part, jnp.bfloat16),
        scratch_shapes=[
            pltpu.VMEM((2,) + part, jnp.float32),
            pltpu.VMEM(part, jnp.float32),
            pltpu.VMEM(part, jnp.float32),
            pltpu.VMEM(part, jnp.float32),
            pltpu.VMEM((rings - 1,) + part[1:], jnp.float32),
            count,
            count,
        ],
        compiler_params=pltpu.CompilerParams(
            collective_id=2, has_side_effects=True, vmem_limit_bytes=VMEM_BYTES
        ),
    )(grads.reshape((2, 2) + part))


def put_pairs(pairs, tap):
    channels = pairs.shape[1] // 2
    pairs[...] = jnp.zeros_like(pairs)
    for k in range(9):
        weights = tap(k)
        pairs[k * channels : (k + 1) * channels, :channels] = weights
        pairs[(k + 3) * channels : (k + 4) * channels, channels:] = weights


def tap_reader(weights, view):
    channels = weights.shape[2]
    return lambda k: weights[view, k * channels : (k + 1) * channels, :]


def put_shifts(padded, frame, values):
    half, _, side, channels = values.shape
    rounded = values.astype(jnp.bfloat16)
    wide = rounded.astype(jnp.float32).reshape(2 * half, side, channels)
    column = lax.broadcasted_iota(jnp.int32, (1, side, channels), 1)
    left = jnp.where(column == 0, 0.0, pltpu.roll(wide, 1, 1)).astype(jnp.bfloat16)
    right = jnp.where(column == side - 1, 0.0, pltpu.roll(wide, side - 1, 1)).astype(jnp.bfloat16)
    for at, part in enumerate((left, rounded, right)):
        part = part.reshape(values.shape)
        lanes = slice(at * channels, (at + 1) * channels)
        padded[frame, 0:half, 1, :, lanes] = part[:, 0]
        padded[frame, 1 : half + 1, 0, :, lanes] = part[:, 1]
    return rounded


def four_rows(padded):
    half = padded.shape[1] - 1
    stacked = jnp.concatenate(
        [padded[:, 0:half, 0], padded[:, 0:half, 1], padded[:, 1:, 0], padded[:, 1:, 1]], axis=-1
    )
    return stacked.reshape(-1, stacked.shape[-1])


def conv_rows(padded, pairs):
    out = jnp.dot(four_rows(padded), pairs[...], preferred_element_type=jnp.float32)
    channels = pairs.shape[1] // 2
    shape = (padded.shape[0], padded.shape[1] - 1, padded.shape[3], channels)
    return (out[:, :channels].reshape(shape), out[:, channels:].reshape(shape))


def clear_edges(padded):
    shape = padded.shape
    none = jnp.zeros((shape[0],) + shape[3:], padded.dtype)
    padded[:, 0, 0] = none
    padded[:, shape[1] - 1, 1] = none


def sigmoid(values):
    return 0.5 + 0.5 * jnp.tanh(0.5 * values)


def forward_kernel(
    maps,
    in_w,
    out_w,
    decay,
    skip,
    states_b,
    slope,
    pooled,
    in_pairs,
    out_pairs,
    padded,
    inputs,
    carried,
):
    step = pl.program_id(0)
    view = lax.axis_index("tm") // (lax.axis_size("tm") // 2)

    @pl.when(step == 0)
    def _():
        put_pairs(in_pairs, tap_reader(in_w, view))
        put_pairs(out_pairs, tap_reader(out_w, view))
        clear_edges(padded)
        carried[...] = jnp.zeros_like(carried)
        pooled[...] = jnp.zeros_like(pooled)

    for frame in range(maps.shape[0]):
        put_shifts(padded, frame, maps[frame])
    even, odd = conv_rows(padded, in_pairs)
    inputs[:, :, 0] = even.astype(jnp.bfloat16)
    inputs[:, :, 1] = odd.astype(jnp.bfloat16)
    for frame in range(maps.shape[0]):
        now = decay[frame : frame + 1, :].reshape(1, 1, 1, -1)
        state = now * carried[...] + inputs[frame].astype(jnp.float32)
        carried[...] = state
        states_b[frame] = put_shifts(padded, frame, state)
    gain = skip[pl.ds(view, 1), :].reshape(1, 1, 1, -1)
    total = pooled[...]
    for parity, out in enumerate(conv_rows(padded, out_pairs)):
        value = out + gain * inputs[:, :, parity].astype(jnp.float32)
        sigma = sigmoid(value)
        active = value * sigma
        slope[:, :, parity] = sigma + active * (1.0 - sigma)
        total = total + jnp.sum(active.reshape(-1, 8, active.shape[-1]), axis=0)
    pooled[...] = total


def backward_kernel(
    maps,
    states_b,
    slope,
    dpooled,
    out_w,
    decay,
    skip,
    grads,
    pairs,
    padded,
    dmix,
    total,
    carried,
):
    step, steps = (pl.program_id(0), pl.num_programs(0))
    me, peers = (lax.axis_index("tm"), lax.axis_size("tm"))
    view = me // (peers // 2)
    block, half, _, side, channels = maps.shape
    frames = decay.shape[0]

    @pl.when(step == 0)
    def _():
        read = tap_reader(out_w, view)
        put_pairs(pairs, lambda k: read(8 - k).astype(jnp.float32).T.astype(jnp.bfloat16))
        clear_edges(padded)
        carried[...] = jnp.zeros_like(carried)
        total[...] = jnp.zeros_like(total)

    def tap_product(values):
        both = jnp.concatenate([values[:, :, 0], values[:, :, 1]], axis=-1)
        return lax.dot_general(
            both.reshape(-1, 2 * channels),
            four_rows(padded),
            (((0,), (0,)), ((), ())),
            preferred_element_type=jnp.float32,
        )

    row = lax.axis_index("batch") * peers + me
    share = (dpooled[pl.ds(row, 1), :] / (frames * 2 * half * side)).reshape(1, 1, 1, -1)
    gain = skip[pl.ds(view, 1), :].reshape(1, 1, 1, -1)
    for frame in range(block):
        part = share * slope[frame]
        dmix[frame] = gain * part
        put_shifts(padded, frame, part)
    total[1] += tap_product(states_b[...])
    even, odd = conv_rows(padded, pairs)
    first = (steps - 1 - step) * block
    for frame in reversed(range(block)):
        now = decay[pl.ds(jnp.minimum(first + frame + 1, frames - 1), 1), :].reshape(1, 1, -1)
        for parity, out in enumerate((even, odd)):
            adjoint = out[frame] + now * carried[:, parity]
            carried[:, parity] = adjoint
            dmix[frame, :, parity] += adjoint
        put_shifts(padded, frame, dmix[frame])
    total[0] += tap_product(maps[...])

    @pl.when(step == steps - 1)
    def _():
        for which in range(2):
            for row_off in range(3):
                for col_off in range(3):
                    tap = 3 * row_off + col_off
                    summed = 0.0
                    for parity in range(2):
                        at = (3 * (2 + parity - row_off) + 2 - col_off) * channels
                        summed += total[
                            which, parity * channels : (parity + 1) * channels, at : at + channels
                        ]
                    grads[which, tap * channels : (tap + 1) * channels, :] = summed


def middle_kernel(cells, everyone, proj_in, gain, proj_out, dpooled):
    rings, peers, _, channels = everyone.shape
    rows, per_view = (rings * peers, peers // 2)
    clips = rings * per_view
    width = proj_out.shape[1]
    pooled = (jnp.sum(everyone[...], axis=2) / cells).reshape(rows, channels)
    place = lax.broadcasted_iota(jnp.int32, (rows, width), 0)
    rgb = lax.rem(place, peers) < per_view

    def mean(values):
        of_rgb = jnp.sum(jnp.where(rgb, values, 0.0), axis=0, keepdims=True) / clips
        of_flow = jnp.sum(jnp.where(rgb, 0.0, values), axis=0, keepdims=True) / clips
        return jnp.where(rgb, of_rgb, of_flow)

    def normed(values):
        centered = values - mean(values)
        scale = lax.rsqrt(mean(centered * centered) + EPSILON)
        return (centered * scale, scale)

    def backed(grad, values, scale):
        return (grad - mean(grad) - values * mean(grad * values)) * scale

    hidden = jnp.dot(pooled, proj_in[...], precision=HIGHEST, preferred_element_type=jnp.float32)
    hidden_x, hidden_s = normed(hidden)
    hidden_n = hidden_x * gain[...]
    relu_b = jnp.maximum(hidden_n, 0.0).astype(jnp.bfloat16)
    z_x, z_s = normed(jnp.dot(relu_b, proj_out[...], preferred_element_type=jnp.float32))
    z_n = z_x.astype(jnp.bfloat16).astype(jnp.float32)
    other = pltpu.roll(z_n.reshape(rings, peers, width), per_view, 1).reshape(rows, width)
    agree = jnp.sum(jnp.where(rgb, z_n * other, 0.0), axis=0, keepdims=True) / clips
    extra = -2.0 * (1.0 - agree) - 2.0 * LAMBDA_OFF * agree
    other_b = other.astype(jnp.bfloat16)
    gram = lax.dot_general(
        other_b, other_b, (((1,), (1,)), ((), ())), preferred_element_type=jnp.float32
    )
    down = lax.rem(lax.broadcasted_iota(jnp.int32, (rows, rows), 0), peers) < per_view
    along = lax.rem(lax.broadcasted_iota(jnp.int32, (rows, rows), 1), peers) < per_view
    gram = jnp.where(down == along, gram, 0.0) * (2.0 * LAMBDA_OFF / clips)
    spread = jnp.dot(gram, z_n, precision=HIGHEST, preferred_element_type=jnp.float32)
    dz = backed((spread + other * extra) / clips, z_x, z_s)
    drelu = lax.dot_general(
        dz.astype(jnp.bfloat16),
        proj_out[...],
        (((1,), (1,)), ((), ())),
        preferred_element_type=jnp.float32,
    )
    dhidden = backed(jnp.where(hidden_n > 0, drelu, 0.0) * gain[...], hidden_x, hidden_s)
    dpooled[...] = lax.dot_general(
        dhidden,
        proj_in[...],
        (((1,), (1,)), ((), ())),
        precision=HIGHEST,
        preferred_element_type=jnp.float32,
    )


def forward(maps, in_w, out_w, decay, skip):
    frames, half, _, side, channels = maps.shape
    shape = (BLOCK, half, 2, side, channels)
    frame_spec = pl.BlockSpec(shape, lambda i: (i, 0, 0, 0, 0))
    whole = pl.BlockSpec(memory_space=pltpu.VMEM)
    pairs = pltpu.VMEM((12 * channels, 2 * channels), jnp.bfloat16)
    return pl.pallas_call(
        forward_kernel,
        grid=(frames // BLOCK,),
        in_specs=[
            frame_spec,
            whole,
            whole,
            pl.BlockSpec((BLOCK, channels), lambda i: (i, 0)),
            whole,
        ],
        out_specs=[frame_spec, frame_spec, whole],
        out_shape=[
            jax.ShapeDtypeStruct(maps.shape, jnp.bfloat16),
            jax.ShapeDtypeStruct(maps.shape, jnp.float32),
            jax.ShapeDtypeStruct((8, channels), jnp.float32),
        ],
        scratch_shapes=[
            pairs,
            pairs,
            pltpu.VMEM((BLOCK, half + 1, 2, side, 3 * channels), jnp.bfloat16),
            pltpu.VMEM(shape, jnp.bfloat16),
            pltpu.VMEM(shape[1:], jnp.float32),
        ],
        compiler_params=pltpu.CompilerParams(vmem_limit_bytes=VMEM_BYTES),
    )(maps, in_w, out_w, decay, skip)


def backward(maps, states_b, slope, dpooled, out_w, decay, skip):
    frames, half, _, side, channels = maps.shape
    steps = frames // BLOCK
    shape = (BLOCK, half, 2, side, channels)
    frame_spec = pl.BlockSpec(shape, lambda i: (steps - 1 - i, 0, 0, 0, 0))
    whole = pl.BlockSpec(memory_space=pltpu.VMEM)
    return pl.pallas_call(
        backward_kernel,
        grid=(steps,),
        in_specs=[frame_spec, frame_spec, frame_spec, whole, whole, whole, whole],
        out_specs=whole,
        out_shape=jax.ShapeDtypeStruct((2, 9 * channels, channels), jnp.float32),
        scratch_shapes=[
            pltpu.VMEM((12 * channels, 2 * channels), jnp.bfloat16),
            pltpu.VMEM((BLOCK, half + 1, 2, side, 3 * channels), jnp.bfloat16),
            pltpu.VMEM(shape, jnp.float32),
            pltpu.VMEM((2, 2 * channels, 12 * channels), jnp.float32),
            pltpu.VMEM(shape[1:], jnp.float32),
        ],
        compiler_params=pltpu.CompilerParams(vmem_limit_bytes=VMEM_BYTES),
    )(maps, states_b, slope, dpooled, out_w, decay, skip)


def middle(everyone, cells, proj_in, proj_gain, proj_out):
    rings, peers, _, channels = everyone.shape
    whole = pl.BlockSpec(memory_space=pltpu.VMEM)
    return pl.pallas_call(
        functools.partial(middle_kernel, cells),
        in_specs=[whole] * 4,
        out_specs=whole,
        out_shape=jax.ShapeDtypeStruct((rings * peers, channels), jnp.float32),
        compiler_params=pltpu.CompilerParams(vmem_limit_bytes=VMEM_BYTES),
    )(everyone, proj_in, proj_gain[None], proj_out)


def clip_per_device(
    rgb_maps, flow_maps, in_weights, out_weights, decay, skip, proj_in, proj_gain, proj_out
):
    side, channels = rgb_maps.shape[-2:]
    maps, decays = exchange(rgb_maps, flow_maps, decay)
    frames = maps.shape[0]
    maps = maps.reshape(frames, side // 2, 2, side, channels)
    states_b, slope, pooled = forward(maps, in_weights, out_weights, decays, skip)
    dpooled = middle(gather(pooled), frames * side * side, proj_in, proj_gain, proj_out)
    grads = backward(maps, states_b, slope, dpooled, out_weights, decays, skip)
    whole = reduce_grads(grads.reshape(-1, channels)).astype(jnp.float32)
    whole = whole.reshape(2, 2, 9 * channels, channels)
    return (whole[:, 0], whole[:, 1])


def per_device(rgb_maps, *others):
    clips, frames_here, side = rgb_maps.shape[:3]
    fits = lax.axis_size("tm") == 2 * clips and side % 2 == 0
    fits = fits and clips == 4 and (9 * rgb_maps.shape[-1]) % (32 * lax.axis_size("batch")) == 0
    fits = fits and (frames_here * lax.axis_size("tm")) % BLOCK == 0
    chosen = clip_per_device if fits else scanned_per_device
    return chosen(rgb_maps, *others)


def solution(mesh):
    return jax.shard_map(
        per_device,
        mesh=mesh,
        in_specs=(
            P("batch", "tm", None, None, None),
            P("batch", "tm", None, None, None),
            P(),
            P(),
            P(None, "tm", None),
            P(),
            P(),
            P(),
            P(),
        ),
        out_specs=(P(), P()),
        check_vma=False,
    )
```

```python
import functools

import jax
import jax.numpy as jnp
from jax import lax
from jax.experimental import pallas as pl
from jax.experimental.pallas import tpu as pltpu
from jax.sharding import PartitionSpec as P

LAMBDA_OFF = 0.0051
EPSILON = 1e-05
HIGHEST = lax.Precision.HIGHEST


def prefix(x, axis, combine, identity, reverse):
    peers, here = (lax.axis_size(axis), lax.axis_index(axis))
    everything = jax.tree.map(lambda part: lax.all_gather(part, axis), x)
    start = jax.tree.map(
        lambda part, zero: jnp.broadcast_to(jnp.asarray(zero, part.dtype), part.shape), x, identity
    )

    def lap(k, before):
        at = peers - 1 - k if reverse else k
        reached = at > here if reverse else at < here
        new = combine(before, jax.tree.map(lambda part: part[at], everything))
        return jax.tree.map(lambda a, b: jnp.where(reached, a, b), new, before)

    return lax.fori_loop(0, peers, lap, start)


def patches(feature_maps, flip_sign):
    map_side = feature_maps.shape[-2]
    padding = [(0, 0)] * (feature_maps.ndim - 3) + [(1, 1), (1, 1), (0, 0)]
    padded = jnp.pad(feature_maps, padding)
    pieces = []
    for row_off in range(3):
        for col_off in range(3):
            top_row = 1 + flip_sign * (row_off - 1)
            left_col = 1 + flip_sign * (col_off - 1)
            pieces.append(
                padded[..., top_row : top_row + map_side, left_col : left_col + map_side, :]
            )
    return jnp.concatenate(pieces, axis=-1)


def convolve(feature_maps, weights, flip_sign):
    stacked = patches(feature_maps, flip_sign)
    flat = stacked.reshape(-1, stacked.shape[-1])
    result = jnp.dot(flat, weights, preferred_element_type=jnp.float32)
    return result.reshape(feature_maps.shape[:-1] + (weights.shape[1],))


def flipped(weights):
    channels = weights.shape[1]
    return weights.reshape(9, channels, channels).transpose(0, 2, 1).reshape(9 * channels, channels)


def weight_product(feature_maps, grads):
    stacked = patches(feature_maps, 1)
    flat = stacked.reshape(-1, stacked.shape[-1])
    return lax.dot_general(
        flat,
        grads.reshape(-1, grads.shape[-1]),
        (((0,), (0,)), ((), ())),
        preferred_element_type=jnp.float32,
    )


def silu_grad(values):
    sigma = jax.nn.sigmoid(values)
    return sigma * (1.0 + values * (1.0 - sigma))


def compose(earlier, latter):
    return (earlier[0] * latter[0], latter[0] * earlier[1] + latter[1])


def compose_pair(earlier, latter):
    first_view = compose((earlier[0], earlier[1]), (latter[0], latter[1]))
    second_view = compose((earlier[2], earlier[3]), (latter[2], latter[3]))
    return (first_view[0], first_view[1], second_view[0], second_view[1])


def local_states(view_maps, in_w, decays):
    inputs = convolve(view_maps, in_w, 1).astype(jnp.bfloat16)
    frames_here = view_maps.shape[1]
    carried = jnp.zeros(view_maps.shape[:1] + view_maps.shape[2:], jnp.float32)
    collected = []
    for frame_idx in range(frames_here):
        carried = decays[frame_idx] * carried + inputs[:, frame_idx].astype(jnp.float32)
        collected.append(carried)
    return (inputs, jnp.stack(collected, axis=1), jnp.prod(decays, axis=0), carried)


def finish_states(inputs, partial_states, decays, incoming, out_w, skip_v):
    running = jnp.cumprod(decays, axis=0)
    states = partial_states + running[None, :, None, None, :] * incoming[:, None]
    states_b = states.astype(jnp.bfloat16)
    mixed_out = convolve(states_b, out_w, 1) + skip_v * inputs.astype(jnp.float32)
    pooled_part = jnp.sum(jax.nn.silu(mixed_out), axis=(1, 2, 3))
    return (states_b, mixed_out, pooled_part)


def local_adjoint(dpool, mixed_out, states_b, decays, out_w, cell_count):
    dmix = dpool[:, None, None, None, :] / cell_count * silu_grad(mixed_out)
    dmix_b = dmix.astype(jnp.bfloat16)
    out_grad = weight_product(states_b, dmix_b)
    from_out = convolve(dmix_b, flipped(out_w), -1)
    frames_here = mixed_out.shape[1]
    adjoint_list = [None] * frames_here
    carried = from_out[:, frames_here - 1]
    adjoint_list[frames_here - 1] = carried
    for frame_idx in range(frames_here - 2, -1, -1):
        carried = from_out[:, frame_idx] + decays[frame_idx + 1] * carried
        adjoint_list[frame_idx] = carried
    partial_adjoint = jnp.stack(adjoint_list, axis=1)
    return (dmix, out_grad, partial_adjoint, decays[0] * partial_adjoint[:, 0])


def finish_adjoint(view_maps, dmix, partial_adjoint, decays, incoming, skip_v):
    reversed_prod = jnp.cumprod(decays[::-1], axis=0)[::-1]
    after_prod = jnp.concatenate(
        [reversed_prod[1:], jnp.ones((1, decays.shape[1]), jnp.float32)], axis=0
    )
    adjoint = partial_adjoint + after_prod[None, :, None, None, :] * incoming[:, None]
    dinput = (adjoint + skip_v * dmix).astype(jnp.bfloat16)
    return weight_product(view_maps, dinput)


def barlow_grads(corr_rows, first_row):
    row_ids = jnp.arange(corr_rows.shape[0]) + first_row
    eye_mask = row_ids[:, None] == jnp.arange(corr_rows.shape[1])[None, :]
    return jnp.where(eye_mask, -2.0 * (1.0 - corr_rows), 2.0 * LAMBDA_OFF * corr_rows)


def scanned_per_device(
    rgb_maps, flow_maps, in_weights, out_weights, decay, skip, proj_in, proj_gain, proj_out
):
    channels = rgb_maps.shape[-1]
    state_shape = rgb_maps.shape[:1] + rgb_maps.shape[2:]
    unit_decay = jnp.ones((channels,), jnp.float32)
    zero_state = jnp.zeros(state_shape, jnp.float32)
    cell_count = rgb_maps.shape[1] * lax.axis_size("tm") * rgb_maps.shape[2] * rgb_maps.shape[3]
    clip_total = rgb_maps.shape[0] * lax.axis_size("batch")
    in_rgb, part_rgb, total_rgb, end_rgb = local_states(rgb_maps, in_weights[0], decay[0])
    in_flow, part_flow, total_flow, end_flow = local_states(flow_maps, in_weights[1], decay[1])
    scanned = prefix(
        (total_rgb, end_rgb, total_flow, end_flow),
        "tm",
        compose_pair,
        (unit_decay, zero_state, unit_decay, zero_state),
        False,
    )
    income_rgb = scanned[1]
    income_flow = scanned[3]
    states_rgb, mixed_rgb, pooled_rgb = finish_states(
        in_rgb, part_rgb, decay[0], income_rgb, out_weights[0], skip[0]
    )
    states_flow, mixed_flow, pooled_flow = finish_states(
        in_flow, part_flow, decay[1], income_flow, out_weights[1], skip[1]
    )
    pooled_sums = lax.psum((pooled_rgb, pooled_flow), "tm")
    pooled_views = (pooled_sums[0] / cell_count, pooled_sums[1] / cell_count)
    hidden_views = [
        jnp.dot(
            pooled_views[view_idx], proj_in, precision=HIGHEST, preferred_element_type=jnp.float32
        )
        for view_idx in range(2)
    ]
    hidden_totals = lax.psum(
        (jnp.sum(hidden_views[0], axis=0), jnp.sum(hidden_views[1], axis=0)), "batch"
    )
    hidden_cent = [
        hidden_views[view_idx] - hidden_totals[view_idx] / clip_total for view_idx in range(2)
    ]
    hidden_squares = lax.psum(
        (
            jnp.sum(hidden_cent[0] * hidden_cent[0], axis=0),
            jnp.sum(hidden_cent[1] * hidden_cent[1], axis=0),
        ),
        "batch",
    )
    hidden_scale = [
        lax.rsqrt(hidden_squares[view_idx] / clip_total + EPSILON) for view_idx in range(2)
    ]
    hidden_x = [hidden_cent[view_idx] * hidden_scale[view_idx] for view_idx in range(2)]
    hidden_n = [hidden_x[view_idx] * proj_gain for view_idx in range(2)]
    z_views = [
        jnp.dot(
            jnp.maximum(hidden_n[view_idx], 0.0).astype(jnp.bfloat16),
            proj_out,
            preferred_element_type=jnp.float32,
        )
        for view_idx in range(2)
    ]
    z_totals = lax.psum((jnp.sum(z_views[0], axis=0), jnp.sum(z_views[1], axis=0)), "batch")
    z_cent = [z_views[view_idx] - z_totals[view_idx] / clip_total for view_idx in range(2)]
    z_squares = lax.psum(
        (jnp.sum(z_cent[0] * z_cent[0], axis=0), jnp.sum(z_cent[1] * z_cent[1], axis=0)), "batch"
    )
    z_scale = [lax.rsqrt(z_squares[view_idx] / clip_total + EPSILON) for view_idx in range(2)]
    z_x = [z_cent[view_idx] * z_scale[view_idx] for view_idx in range(2)]
    zn_rgb = z_x[0].astype(jnp.bfloat16)
    zn_flow = z_x[1].astype(jnp.bfloat16)
    proj_width = proj_out.shape[1]
    row_block = proj_width // lax.axis_size("tm")
    first_row = lax.axis_index("tm") * row_block
    own_block = lax.dynamic_slice_in_dim(zn_rgb, first_row, row_block, 1)
    gathered_block, gathered_flow = (
        lax.all_gather(own_block, "batch", axis=0, tiled=True),
        lax.all_gather(zn_flow, "batch", axis=0, tiled=True),
    )
    corr_block = (
        lax.dot_general(
            gathered_block,
            gathered_flow,
            (((0,), (0,)), ((), ())),
            preferred_element_type=jnp.float32,
        )
        / clip_total
    )
    grad_block = barlow_grads(corr_block, first_row)
    flow_wide = zn_flow.astype(jnp.float32)
    block_wide = own_block.astype(jnp.float32)
    dzn_cols = (
        lax.dot_general(flow_wide, grad_block, (((1,), (1,)), ((), ())), precision=HIGHEST)
        / clip_total
    )
    dzn_rgb = lax.all_gather(dzn_cols, "tm", axis=1, tiled=True)
    dzn_flow = lax.psum(jnp.dot(block_wide, grad_block, precision=HIGHEST) / clip_total, "tm")
    dzn_views = (dzn_rgb, dzn_flow)
    z_back = lax.psum(
        (
            jnp.sum(dzn_rgb, axis=0),
            jnp.sum(dzn_rgb * z_x[0], axis=0),
            jnp.sum(dzn_flow, axis=0),
            jnp.sum(dzn_flow * z_x[1], axis=0),
        ),
        "batch",
    )
    dxh_views = []
    for view_idx in range(2):
        dz_b = (
            (
                dzn_views[view_idx]
                - z_back[2 * view_idx] / clip_total
                - z_x[view_idx] * (z_back[2 * view_idx + 1] / clip_total)
            )
            * z_scale[view_idx]
        ).astype(jnp.bfloat16)
        drelu = lax.dot_general(
            dz_b, proj_out, (((1,), (1,)), ((), ())), preferred_element_type=jnp.float32
        )
        dxh_views.append(jnp.where(hidden_n[view_idx] > 0, drelu, 0.0) * proj_gain)
    h_back = lax.psum(
        (
            jnp.sum(dxh_views[0], axis=0),
            jnp.sum(dxh_views[0] * hidden_x[0], axis=0),
            jnp.sum(dxh_views[1], axis=0),
            jnp.sum(dxh_views[1] * hidden_x[1], axis=0),
        ),
        "batch",
    )
    dpooled = []
    for view_idx in range(2):
        dhidden = (
            dxh_views[view_idx]
            - h_back[2 * view_idx] / clip_total
            - hidden_x[view_idx] * (h_back[2 * view_idx + 1] / clip_total)
        ) * hidden_scale[view_idx]
        dpooled.append(
            lax.dot_general(dhidden, proj_in, (((1,), (1,)), ((), ())), precision=HIGHEST)
        )
    dmix_rgb, out_grad_rgb, adj_rgb, send_rgb = local_adjoint(
        dpooled[0], mixed_rgb, states_rgb, decay[0], out_weights[0], cell_count
    )
    dmix_flow, out_grad_flow, adj_flow, send_flow = local_adjoint(
        dpooled[1], mixed_flow, states_flow, decay[1], out_weights[1], cell_count
    )
    returned = prefix(
        (total_rgb, send_rgb, total_flow, send_flow),
        "tm",
        compose_pair,
        (unit_decay, zero_state, unit_decay, zero_state),
        True,
    )
    back_rgb = returned[1]
    back_flow = returned[3]
    in_grad_rgb = finish_adjoint(rgb_maps, dmix_rgb, adj_rgb, decay[0], back_rgb, skip[0])
    in_grad_flow = finish_adjoint(flow_maps, dmix_flow, adj_flow, decay[1], back_flow, skip[1])
    in_stack = jnp.stack([in_grad_rgb, in_grad_flow])
    out_stack = jnp.stack([out_grad_rgb, out_grad_flow])
    shares = (
        lax.psum_scatter(in_stack, "tm", scatter_dimension=1, tiled=True),
        lax.psum_scatter(out_stack, "tm", scatter_dimension=1, tiled=True),
    )
    share_sums = lax.psum((shares[0], shares[1]), "batch")
    whole = (
        lax.all_gather(share_sums[0], "tm", axis=1, tiled=True),
        lax.all_gather(share_sums[1], "tm", axis=1, tiled=True),
    )
    return (whole[0], whole[1])


BLOCK = 16
PARTS = 4
FORWARD_BYTES = 20 * 1024 * 1024
MIDDLE_BYTES = 16 * 1024 * 1024
BACKWARD_BYTES = 24 * 1024 * 1024
SMALL_BYTES = 4 * 1024 * 1024


MESH = pl.DeviceIdType.MESH


def greet(places):
    barrier = pltpu.get_barrier_semaphore()
    for place in places:
        pl.semaphore_signal(barrier, inc=1, device_id=place, device_id_type=MESH)
    pl.semaphore_wait(barrier, len(places))


def exchange_kernel(rgb, flow, decay, maps, decays, send, recv, send_decay, recv_decay, own):
    me, peers = (lax.axis_index("tm"), lax.axis_size("tm"))
    clips, frames = rgb.shape[:2]
    here = pl.ds(pl.multiple_of(me * frames, frames), frames)
    others = [lax.rem(me + k, peers) for k in range(1, peers)]
    greet([{"tm": other} for other in others])
    for view, source in enumerate((rgb, flow)):

        @pl.when(me // clips == view)
        def _(source=source):
            pltpu.make_async_copy(source.at[lax.rem(me, clips)], maps.at[here], own.at[0]).start()

    kept = pltpu.make_async_copy(decay.at[me // clips], decays.at[here], own.at[1])
    kept.start()
    copies = []
    for k, other in enumerate(others):
        for view, source in enumerate((rgb, flow)):
            copy = pltpu.make_async_remote_copy(
                src_ref=source.at[lax.rem(other, clips)],
                dst_ref=maps.at[here],
                send_sem=send.at[k],
                recv_sem=recv.at[k],
                device_id={"tm": other},
                device_id_type=MESH,
            )

            @pl.when(other // clips == view)
            def _(copy=copy):
                copy.start()

        copies.append(copy)
        small = pltpu.make_async_remote_copy(
            src_ref=decay.at[other // clips],
            dst_ref=decays.at[here],
            send_sem=send_decay.at[k],
            recv_sem=recv_decay.at[k],
            device_id={"tm": other},
            device_id_type=MESH,
        )
        small.start()
        copies.append(small)
    for copy in copies:
        copy.wait()
    pltpu.make_async_copy(rgb.at[0], maps.at[here], own.at[0]).wait()
    kept.wait()


def exchange(rgb_maps, flow_maps, decay):
    clips, frames = rgb_maps.shape[:2]
    peers = lax.axis_size("tm")
    channels = decay.shape[-1]
    others = pltpu.SemaphoreType.DMA((peers - 1,))
    return pl.pallas_call(
        exchange_kernel,
        in_specs=[pl.BlockSpec(memory_space=pltpu.HBM)] * 3,
        out_specs=[pl.BlockSpec(memory_space=pl.ANY)] * 2,
        out_shape=[
            jax.ShapeDtypeStruct((frames * peers,) + rgb_maps.shape[2:], rgb_maps.dtype),
            jax.ShapeDtypeStruct((frames * peers, channels), decay.dtype),
        ],
        scratch_shapes=[others, others, others, others, pltpu.SemaphoreType.DMA((2,))],
        compiler_params=pltpu.CompilerParams(
            collective_id=0, has_side_effects=True, vmem_limit_bytes=SMALL_BYTES
        ),
    )(rgb_maps, flow_maps, decay)


def gather_kernel(pooled, everyone, send, recv):
    me, peers = (lax.axis_index("tm"), lax.axis_size("tm"))
    ring, rings = (lax.axis_index("batch"), lax.axis_size("batch"))
    near = [{"tm": lax.rem(me + k, peers)} for k in range(1, peers)]
    far = [{"batch": lax.rem(ring + k, rings)} for k in range(1, rings)]
    greet(near + far)
    everyone[ring, me] = pooled[...]
    copies = []
    for wave, part in ((near, everyone.at[ring, me]), (far, everyone.at[ring])):
        started = []
        for place in wave:
            at = len(copies) + len(started)
            copy = pltpu.make_async_remote_copy(
                src_ref=part,
                dst_ref=part,
                send_sem=send.at[at],
                recv_sem=recv.at[at],
                device_id=place,
                device_id_type=MESH,
            )
            copy.start()
            started.append(copy)
        for copy in started:
            copy.wait_recv()
        copies += started
    for copy in copies:
        copy.wait_send()


def gather(pooled):
    peers, rings = (lax.axis_size("tm"), lax.axis_size("batch"))
    count = pltpu.SemaphoreType.DMA((peers + rings - 2,))
    return pl.pallas_call(
        gather_kernel,
        in_specs=[pl.BlockSpec(memory_space=pltpu.VMEM)],
        out_specs=pl.BlockSpec(memory_space=pltpu.VMEM),
        out_shape=jax.ShapeDtypeStruct((rings, peers) + pooled.shape, pooled.dtype),
        scratch_shapes=[count, count],
        compiler_params=pltpu.CompilerParams(
            collective_id=1, has_side_effects=True, vmem_limit_bytes=SMALL_BYTES
        ),
    )(pooled)


def reduce_kernel(grads, whole, from_core, to_x, from_x, acc, to_ring, from_ring, send, recv):
    me, ring, rings = (lax.axis_index("tm"), lax.axis_index("batch"), lax.axis_size("batch"))
    core, x, y = (lax.rem(me, 2), lax.rem(me // 2, 2), me // 4)
    sibling, across, beyond = (
        {"tm": me + 1 - 2 * core},
        {"tm": me + 2 - 4 * x},
        {"tm": me + 4 - 8 * y},
    )
    others = [lax.rem(ring + k, rings) for k in range(1, rings)]
    greet([sibling, across, beyond] + [{"batch": other} for other in others])
    started = []

    def push(source, target, place):
        at = len(started)
        copy = pltpu.make_async_remote_copy(
            src_ref=source,
            dst_ref=target,
            send_sem=send.at[at],
            recv_sem=recv.at[at],
            device_id=place,
            device_id_type=MESH,
        )
        copy.start()
        started.append(copy)
        return copy

    passed = push(grads.at[1 - core, 1 - x], from_core.at[0], sibling)
    kept = push(grads.at[1 - core, x], from_core.at[1], sibling)
    passed.wait_recv()
    to_x[...] = (grads[core, 1 - x] + from_core[0]).astype(to_x.dtype)
    crossed = push(to_x, from_x, across)
    kept.wait_recv()
    acc[...] = grads[core, x] + from_core[1]
    crossed.wait_recv()
    acc[...] += from_x[...].astype(jnp.float32)
    to_ring[...] = acc[...].astype(to_ring.dtype)
    arrivals = [
        push(to_ring.at[other], from_ring.at[k], {"batch": other})
        for k, other in enumerate(others)
    ]
    total = acc[ring]
    for k, copy in enumerate(arrivals):
        copy.wait_recv()
        total = total + from_ring[k].astype(jnp.float32)
    whole[y, core, x, ring] = total.astype(whole.dtype)
    part = whole.at[y, core, x, ring]
    for copy in [push(part, part, {"batch": other}) for other in others]:
        copy.wait_recv()

    def hand(at_y, at_x, place):
        part = whole.at[at_y, core, at_x]
        return push(part, part, place)

    sideways, upward, inward = (hand(y, x, across), hand(y, x, beyond), [hand(y, x, sibling)])
    sideways.wait_recv()
    corner = hand(y, 1 - x, beyond)
    inward.append(hand(y, 1 - x, sibling))
    upward.wait_recv()
    inward.append(hand(1 - y, x, sibling))
    corner.wait_recv()
    inward.append(hand(1 - y, 1 - x, sibling))
    for copy in inward:
        copy.wait_recv()
    for copy in started:
        copy.wait_send()


def reduce_grads(grads):
    rings = lax.axis_size("batch")
    rows, channels = grads.shape
    part = (rings, rows // (4 * rings), channels)
    count = pltpu.SemaphoreType.DMA((3 + 2 * (rings - 1) + 7,))
    return pl.pallas_call(
        reduce_kernel,
        in_specs=[pl.BlockSpec(memory_space=pltpu.VMEM)],
        out_specs=pl.BlockSpec(memory_space=pltpu.VMEM),
        out_shape=jax.ShapeDtypeStruct((2, 2, 2) + part, jnp.bfloat16),
        scratch_shapes=[
            pltpu.VMEM((2,) + part, jnp.float32),
            pltpu.VMEM(part, jnp.bfloat16),
            pltpu.VMEM(part, jnp.bfloat16),
            pltpu.VMEM(part, jnp.float32),
            pltpu.VMEM(part, jnp.bfloat16),
            pltpu.VMEM((rings - 1,) + part[1:], jnp.bfloat16),
            count,
            count,
        ],
        compiler_params=pltpu.CompilerParams(
            collective_id=2, has_side_effects=True, vmem_limit_bytes=MIDDLE_BYTES
        ),
    )(grads.reshape((2, 2) + part))


def put_pairs(pairs, tap):
    channels = pairs.shape[1] // 2
    pairs[...] = jnp.zeros_like(pairs)
    for k in range(9):
        weights = tap(k)
        pairs[k * channels : (k + 1) * channels, :channels] = weights
        pairs[(k + 3) * channels : (k + 4) * channels, channels:] = weights


def tap_reader(weights, view):
    channels = weights.shape[2]
    return lambda k: weights[view, k * channels : (k + 1) * channels, :]


def put_shifts(padded, frame, values):
    half, _, side, channels = values.shape
    rounded = values.astype(jnp.bfloat16)
    wide = rounded.astype(jnp.float32).reshape(2 * half, side, channels)
    column = lax.broadcasted_iota(jnp.int32, (1, side, channels), 1)
    left = jnp.where(column == 0, 0.0, pltpu.roll(wide, 1, 1)).astype(jnp.bfloat16)
    right = jnp.where(column == side - 1, 0.0, pltpu.roll(wide, side - 1, 1)).astype(jnp.bfloat16)
    for at, part in enumerate((left, rounded, right)):
        part = part.reshape(values.shape)
        lanes = slice(at * channels, (at + 1) * channels)
        padded[frame, 0:half, 1, :, lanes] = part[:, 0]
        padded[frame, 1 : half + 1, 0, :, lanes] = part[:, 1]
    return rounded


def four_rows(padded):
    half = padded.shape[1] - 1
    stacked = jnp.concatenate(
        [padded[:, 0:half, 0], padded[:, 0:half, 1], padded[:, 1:, 0], padded[:, 1:, 1]], axis=-1
    )
    return stacked.reshape(-1, stacked.shape[-1])


def conv_rows(padded, pairs):
    out = jnp.dot(four_rows(padded), pairs[...], preferred_element_type=jnp.float32)
    channels = pairs.shape[1] // 2
    shape = (padded.shape[0], padded.shape[1] - 1, padded.shape[3], channels)
    return (out[:, :channels].reshape(shape), out[:, channels:].reshape(shape))


def clear_edges(padded):
    shape = padded.shape
    none = jnp.zeros((shape[0],) + shape[3:], padded.dtype)
    padded[:, 0, 0] = none
    padded[:, shape[1] - 1, 1] = none


def sigmoid(values):
    return 0.5 + 0.5 * jnp.tanh(0.5 * values)


def forward_kernel(
    maps,
    in_w,
    out_w,
    decay,
    skip,
    states_b,
    slope,
    pooled,
    in_pairs,
    out_pairs,
    padded_in,
    padded_out,
    inputs,
    carried,
):
    step = pl.program_id(0)
    view = lax.axis_index("tm") // (lax.axis_size("tm") // 2)

    @pl.when(step == 0)
    def _():
        put_pairs(in_pairs, tap_reader(in_w, view))
        put_pairs(out_pairs, tap_reader(out_w, view))
        for at in range(PARTS):
            clear_edges(padded_in.at[at])
            clear_edges(padded_out.at[at])
        carried[...] = jnp.zeros_like(carried)
        pooled[...] = jnp.zeros_like(pooled)

    size = maps.shape[0] // PARTS
    parts = [slice(at * size, (at + 1) * size) for at in range(PARTS)]
    gain = skip[pl.ds(view, 1), :].reshape(1, 1, 1, -1)
    for at, part in enumerate(parts):
        for frame in range(size):
            put_shifts(padded_in.at[at], frame, maps[part.start + frame])
        even, odd = conv_rows(padded_in.at[at], in_pairs)
        inputs[part, :, 0] = even.astype(jnp.bfloat16)
        inputs[part, :, 1] = odd.astype(jnp.bfloat16)
    state = carried[...]
    for at, part in enumerate(parts):
        for frame in range(size):
            here = part.start + frame
            now = decay[here : here + 1, :].reshape(1, 1, 1, -1)
            state = now * state + inputs[here].astype(jnp.float32)
            states_b[here] = put_shifts(padded_out.at[at], frame, state)
        mixed = conv_rows(padded_out.at[at], out_pairs)
        for parity, out in enumerate(mixed):
            value = out + gain * inputs[part, :, parity].astype(jnp.float32)
            sigma = sigmoid(value)
            active = value * sigma
            slope[part, :, parity] = sigma + active * (1.0 - sigma)
            pooled[...] += jnp.sum(active.reshape(-1, 8, active.shape[-1]), axis=0)
    carried[...] = state


def backward_kernel(
    maps,
    states_b,
    slope,
    dpooled,
    out_w,
    decay,
    skip,
    grads,
    pairs,
    padded_out,
    padded_in,
    dmix,
    total,
    carried,
):
    step, steps = (pl.program_id(0), pl.num_programs(0))
    me, peers = (lax.axis_index("tm"), lax.axis_size("tm"))
    view = me // (peers // 2)
    block, half, _, side, channels = maps.shape
    frames = decay.shape[0]

    @pl.when(step == 0)
    def _():
        read = tap_reader(out_w, view)
        put_pairs(pairs, lambda k: read(8 - k).astype(jnp.float32).T.astype(jnp.bfloat16))
        for at in range(PARTS):
            clear_edges(padded_in.at[at])
            clear_edges(padded_out.at[at])
        carried[...] = jnp.zeros_like(carried)
        total[...] = jnp.zeros_like(total)

    def tap_product(values, padded):
        both = jnp.concatenate([values[:, :, 0], values[:, :, 1]], axis=-1)
        return lax.dot_general(
            both.reshape(-1, 2 * channels),
            four_rows(padded),
            (((0,), (0,)), ((), ())),
            preferred_element_type=jnp.float32,
        )

    row = lax.axis_index("batch") * peers + me
    share = (dpooled[pl.ds(row, 1), :] / (frames * 2 * half * side)).reshape(1, 1, 1, -1)
    gain = skip[pl.ds(view, 1), :].reshape(1, 1, 1, -1)
    size = block // PARTS
    parts = [(at, slice(at * size, (at + 1) * size)) for at in reversed(range(PARTS))]
    first = (steps - 1 - step) * block
    outs = []
    for at, part in parts:
        for frame in range(size):
            here = part.start + frame
            mixed = share * slope[here]
            dmix[here] = gain * mixed
            put_shifts(padded_out.at[at], frame, mixed)
        outs.append(conv_rows(padded_out.at[at], pairs))
    back = [carried[:, parity] for parity in range(2)]
    for (at, part), out in zip(parts, outs):
        total[1] += tap_product(states_b[part], padded_out.at[at])
        for frame in reversed(range(size)):
            here = part.start + frame
            row = jnp.minimum(first + here + 1, frames - 1)
            now = decay[pl.ds(row, 1), :].reshape(1, 1, -1)
            for parity in range(2):
                back[parity] = out[parity][frame] + now * back[parity]
                dmix[here, :, parity] += back[parity]
            put_shifts(padded_in.at[at], frame, dmix[here])
    for parity in range(2):
        carried[:, parity] = back[parity]
    for at, part in parts:
        total[0] += tap_product(maps[part], padded_in.at[at])

    @pl.when(step == steps - 1)
    def _():
        for which in range(2):
            for row_off in range(3):
                for col_off in range(3):
                    tap = 3 * row_off + col_off
                    summed = 0.0
                    for parity in range(2):
                        at = (3 * (2 + parity - row_off) + 2 - col_off) * channels
                        summed += total[
                            which, parity * channels : (parity + 1) * channels, at : at + channels
                        ]
                    grads[which, tap * channels : (tap + 1) * channels, :] = summed


def middle_kernel(cells, everyone, proj_in, gain, proj_out, dpooled):
    rings, peers, _, channels = everyone.shape
    rows, per_view = (rings * peers, peers // 2)
    clips = rings * per_view
    width = proj_out.shape[1]
    pooled = (jnp.sum(everyone[...], axis=2) / cells).reshape(rows, channels)
    place = lax.broadcasted_iota(jnp.int32, (rows, width), 0)
    rgb = lax.rem(place, peers) < per_view

    def mean(values):
        of_rgb = jnp.sum(jnp.where(rgb, values, 0.0), axis=0, keepdims=True) / clips
        of_flow = jnp.sum(jnp.where(rgb, 0.0, values), axis=0, keepdims=True) / clips
        return jnp.where(rgb, of_rgb, of_flow)

    def normed(values):
        centered = values - mean(values)
        scale = lax.rsqrt(mean(centered * centered) + EPSILON)
        return (centered * scale, scale)

    def backed(grad, values, scale):
        return (grad - mean(grad) - values * mean(grad * values)) * scale

    hidden = jnp.dot(pooled, proj_in[...], precision=HIGHEST, preferred_element_type=jnp.float32)
    hidden_x, hidden_s = normed(hidden)
    hidden_n = hidden_x * gain[...]
    relu_b = jnp.maximum(hidden_n, 0.0).astype(jnp.bfloat16)
    z_x, z_s = normed(jnp.dot(relu_b, proj_out[...], preferred_element_type=jnp.float32))
    z_n = z_x.astype(jnp.bfloat16).astype(jnp.float32)
    other = pltpu.roll(z_n.reshape(rings, peers, width), per_view, 1).reshape(rows, width)
    agree = jnp.sum(jnp.where(rgb, z_n * other, 0.0), axis=0, keepdims=True) / clips
    extra = -2.0 * (1.0 - agree) - 2.0 * LAMBDA_OFF * agree
    other_b = other.astype(jnp.bfloat16)
    gram = lax.dot_general(
        other_b, other_b, (((1,), (1,)), ((), ())), preferred_element_type=jnp.float32
    )
    down = lax.rem(lax.broadcasted_iota(jnp.int32, (rows, rows), 0), peers) < per_view
    along = lax.rem(lax.broadcasted_iota(jnp.int32, (rows, rows), 1), peers) < per_view
    gram = jnp.where(down == along, gram, 0.0) * (2.0 * LAMBDA_OFF / clips)
    spread = jnp.dot(gram, z_n, precision=HIGHEST, preferred_element_type=jnp.float32)
    dz = backed((spread + other * extra) / clips, z_x, z_s)
    drelu = lax.dot_general(
        dz.astype(jnp.bfloat16),
        proj_out[...],
        (((1,), (1,)), ((), ())),
        preferred_element_type=jnp.float32,
    )
    dhidden = backed(jnp.where(hidden_n > 0, drelu, 0.0) * gain[...], hidden_x, hidden_s)
    dpooled[...] = lax.dot_general(
        dhidden,
        proj_in[...],
        (((1,), (1,)), ((), ())),
        precision=HIGHEST,
        preferred_element_type=jnp.float32,
    )


def padded_shape(half, side, channels):
    return pltpu.VMEM((PARTS, BLOCK // PARTS, half + 1, 2, side, 3 * channels), jnp.bfloat16)


def forward(maps, in_w, out_w, decay, skip):
    frames, half, _, side, channels = maps.shape
    shape = (BLOCK, half, 2, side, channels)
    frame_spec = pl.BlockSpec(shape, lambda i: (i, 0, 0, 0, 0))
    whole = pl.BlockSpec(memory_space=pltpu.VMEM)
    pairs = pltpu.VMEM((12 * channels, 2 * channels), jnp.bfloat16)
    return pl.pallas_call(
        forward_kernel,
        grid=(frames // BLOCK,),
        in_specs=[
            frame_spec,
            whole,
            whole,
            pl.BlockSpec((BLOCK, channels), lambda i: (i, 0)),
            whole,
        ],
        out_specs=[frame_spec, frame_spec, whole],
        out_shape=[
            jax.ShapeDtypeStruct(maps.shape, jnp.bfloat16),
            jax.ShapeDtypeStruct(maps.shape, jnp.float32),
            jax.ShapeDtypeStruct((8, channels), jnp.float32),
        ],
        scratch_shapes=[
            pairs,
            pairs,
            padded_shape(half, side, channels),
            padded_shape(half, side, channels),
            pltpu.VMEM(shape, jnp.bfloat16),
            pltpu.VMEM(shape[1:], jnp.float32),
        ],
        compiler_params=pltpu.CompilerParams(vmem_limit_bytes=FORWARD_BYTES),
    )(maps, in_w, out_w, decay, skip)


def backward(maps, states_b, slope, dpooled, out_w, decay, skip):
    frames, half, _, side, channels = maps.shape
    steps = frames // BLOCK
    shape = (BLOCK, half, 2, side, channels)
    frame_spec = pl.BlockSpec(shape, lambda i: (steps - 1 - i, 0, 0, 0, 0))
    whole = pl.BlockSpec(memory_space=pltpu.VMEM)
    return pl.pallas_call(
        backward_kernel,
        grid=(steps,),
        in_specs=[frame_spec, frame_spec, frame_spec, whole, whole, whole, whole],
        out_specs=whole,
        out_shape=jax.ShapeDtypeStruct((2, 9 * channels, channels), jnp.float32),
        scratch_shapes=[
            pltpu.VMEM((12 * channels, 2 * channels), jnp.bfloat16),
            padded_shape(half, side, channels),
            padded_shape(half, side, channels),
            pltpu.VMEM(shape, jnp.float32),
            pltpu.VMEM((2, 2 * channels, 12 * channels), jnp.float32),
            pltpu.VMEM(shape[1:], jnp.float32),
        ],
        compiler_params=pltpu.CompilerParams(vmem_limit_bytes=BACKWARD_BYTES),
    )(maps, states_b, slope, dpooled, out_w, decay, skip)


def middle(everyone, cells, proj_in, proj_gain, proj_out):
    rings, peers, _, channels = everyone.shape
    whole = pl.BlockSpec(memory_space=pltpu.VMEM)
    return pl.pallas_call(
        functools.partial(middle_kernel, cells),
        in_specs=[whole] * 4,
        out_specs=whole,
        out_shape=jax.ShapeDtypeStruct((rings * peers, channels), jnp.float32),
        compiler_params=pltpu.CompilerParams(vmem_limit_bytes=MIDDLE_BYTES),
    )(everyone, proj_in, proj_gain[None], proj_out)


def clip_per_device(
    rgb_maps, flow_maps, in_weights, out_weights, decay, skip, proj_in, proj_gain, proj_out
):
    side, channels = rgb_maps.shape[-2:]
    maps, decays = exchange(rgb_maps, flow_maps, decay)
    frames = maps.shape[0]
    maps = maps.reshape(frames, side // 2, 2, side, channels)
    states_b, slope, pooled = forward(maps, in_weights, out_weights, decays, skip)
    dpooled = middle(gather(pooled), frames * side * side, proj_in, proj_gain, proj_out)
    grads = backward(maps, states_b, slope, dpooled, out_weights, decays, skip)
    whole = reduce_grads(grads.reshape(-1, channels)).astype(jnp.float32)
    whole = whole.reshape(2, 2, 9 * channels, channels)
    return (whole[:, 0], whole[:, 1])


def per_device(rgb_maps, *others):
    clips, frames_here, side = rgb_maps.shape[:3]
    fits = lax.axis_size("tm") == 2 * clips and side % 2 == 0
    fits = fits and clips == 4 and (9 * rgb_maps.shape[-1]) % (32 * lax.axis_size("batch")) == 0
    fits = fits and (frames_here * lax.axis_size("tm")) % BLOCK == 0
    chosen = clip_per_device if fits else scanned_per_device
    return chosen(rgb_maps, *others)


def solution(mesh):
    return jax.shard_map(
        per_device,
        mesh=mesh,
        in_specs=(
            P("batch", "tm", None, None, None),
            P("batch", "tm", None, None, None),
            P(),
            P(),
            P(None, "tm", None),
            P(),
            P(),
            P(),
            P(),
        ),
        out_specs=(P(), P()),
        check_vma=False,
    )
```
